32 devices in a mesh: lat: 2 (over y), lon: 16 (over z, x, core).
Axes of the slice: x: 2, y: 2, z: 4, core: 2. Of those that a mesh axis runs over, the one named last changes fastest.
Arguments:
- signal: bfloat16 [96, 128, 256], P('lat', 'lon'), may hold values from -6 to 6
- cotangent: bfloat16 [96, 128, 256], P('lat', 'lon'), may hold values from -6 to 6
- weights: bfloat16 [4, 256, 256], replicated, may hold values from -0.1875 to 0.1875
- band_kernel: bfloat16 [4, 96, 3, 17], replicated, may hold values from -1.25 to 1.25
- cycle_kernel: bfloat16 [4, 4, 3, 128], replicated, may hold values from -0.3125 to 0.3125
- support_width: int32 [96], replicated, may hold values from 1 to 8, as said below
Outputs:
- conv_output: bfloat16 [96, 128, 256], P('lat', 'lon')
- signal_grad: bfloat16 [96, 128, 256], P('lat', 'lon')
- weight_grad: float32 [4, 256, 256], replicated
The draws below stay inside these ranges and needn't reach their ends.
Inputs may be any that keep to these rules, and one draw needn't show every extreme that they name: `support_width`: some row has the half-width 8.
All inputs are finite; a program needn't handle non-finite values.
Results may differ from the reference program's by a relative error of at most 0.0049.
Values may be sent and summed in bfloat16 or wider, within the bound.
No kernel may reach another device: no remote copies, remote signals or barrier semaphores. Data moves between devices by JAX's collectives and lax.ppermute only.
A program may use at most 64 MiB of HBM per device.

```python
import jax
import jax.numpy as jnp
from jax import lax

C = 256
K = 4
R = 1
H = 8
P_SIZE = 2
NLAT = 96
NLON = 128


def draw_support_width(key, part):
    key = jax.random.fold_in(key, 7)
    first_key, second_key = jax.random.split(key)
    widths = jax.random.randint(first_key, (NLAT,), 1, H + 1, dtype=jnp.int32)
    chosen = jax.random.randint(second_key, (), 0, NLAT, dtype=jnp.int32)
    return jnp.where(jnp.arange(NLAT, dtype=jnp.int32) == chosen, H, widths).astype(jnp.int32)


def shard_levels(own_key, shape, cuts, least, largest):
    level, own = 1.0, jax.random.fold_in(own_key, 6)
    for dim, blocks in cuts:
        steps = jnp.exp(jax.random.uniform(jax.random.fold_in(own, dim), (blocks,), jnp.float32, least / len(cuts), largest / len(cuts)))
        level = level * jnp.repeat(steps, shape[dim] // blocks).reshape([-1 if axis == dim else 1 for axis in range(len(shape))])
    return level


def normal_values(own_key, dims, width, most, cuts=(), held_as=jnp.bfloat16):
    drawn = jax.random.normal(own_key, dims, jnp.float32) * width
    if len(cuts) > 0:
        drawn = shard_levels(own_key, dims, cuts, -0.22, 0.18) * drawn
    return jnp.clip(drawn, min=-most, max=most).astype(held_as)


def setup_inputs(seed: int = 0) -> dict:
    seeds = jax.random.split(jax.random.key(seed), 7)
    return {
        "signal": normal_values(seeds[0], (NLAT, NLON, C), 1.0, 6.0, ((0, 2), (1, 16))),
        "cotangent": normal_values(seeds[1], (NLAT, NLON, C), 1.0, 6.0, ((0, 2), (1, 16))),
        "weights": normal_values(seeds[2], (K, C, C), (K * C) ** -0.5, 0.1875),
        "band_kernel": normal_values(seeds[3], (K, NLAT, 2 * R + 1, 2 * H + 1), ((2 * R + 1) * (H + 1)) ** -0.5, 1.25),
        "cycle_kernel": normal_values(seeds[4], (K, 2 * P_SIZE, 2 * R + 1, NLON), ((2 * R + 1) * NLON) ** -0.5, 0.3125),
        "support_width": draw_support_width(jax.random.fold_in(seeds[6], 71), 0),
    }


precise = lax.Precision.HIGHEST

def band_coefficients(band_kernel, support_width):
    offsets = jnp.abs(jnp.arange(2 * H + 1, dtype=jnp.int32) - H)
    row_ids = jnp.arange(NLAT, dtype=jnp.int32)
    polar_rows = (row_ids < P_SIZE) | (row_ids >= NLAT - P_SIZE)
    allowed = (offsets[None, :] <= support_width[:, None]) & jnp.logical_not(polar_rows)[:, None]
    return band_kernel.astype(jnp.float32) * allowed[None, :, None, :].astype(jnp.float32)

def reference(signal, cotangent, weights, band_kernel, cycle_kernel, support_width):
    coeffs = band_coefficients(band_kernel, support_width)
    coeff_pad = jnp.pad(coeffs, ((0, 0), (R, R), (0, 0), (0, 0)))
    signal_pad = jnp.pad(signal, ((R, R), (0, 0), (0, 0)))
    cot_pad = jnp.pad(cotangent, ((R, R), (0, 0), (0, 0)))
    weights_full = weights.astype(jnp.float32)
    cycle_full = cycle_kernel.astype(jnp.float32)
    lon_ids = jnp.arange(NLON, dtype=jnp.int32)
    circ_index = (lon_ids[:, None] - lon_ids[None, :]) % NLON
    trans_index = (lon_ids[None, :] - lon_ids[:, None]) % NLON

    def band_row(row_index):
        window = lax.dynamic_slice_in_dim(signal_pad, row_index, 2 * R + 1, 0).astype(jnp.float32)
        shifted = jnp.stack([jnp.roll(window, shift_index - H, axis=1) for shift_index in range(2 * H + 1)], axis=1)
        coeff_row = lax.dynamic_index_in_dim(coeffs, row_index, 1, keepdims=False)
        return jnp.einsum('krd,rdlc->klc', coeff_row, shifted, precision=precise)

    def polar_row(row_index):
        pole_row = jnp.where(row_index < P_SIZE, row_index, row_index - NLAT + 2 * P_SIZE)
        window = lax.dynamic_slice_in_dim(signal_pad, row_index, 2 * R + 1, 0).astype(jnp.float32)
        kernel_row = lax.dynamic_index_in_dim(cycle_full, pole_row, 1, keepdims=False)
        circulant = kernel_row[:, :, circ_index]
        return jnp.einsum('krlm,rmc->klc', circulant, window, precision=precise)

    def forward_step(weight_sum, row_index):
        is_polar = (row_index < P_SIZE) | (row_index >= NLAT - P_SIZE)
        filtered = lax.cond(is_polar, polar_row, band_row, row_index)
        filtered = lax.optimization_barrier(filtered.astype(jnp.bfloat16))
        filtered_full = filtered.astype(jnp.float32)
        out_row = jnp.einsum('klc,kce->le', filtered_full, weights_full, precision=precise).astype(jnp.bfloat16)
        cot_row = lax.dynamic_index_in_dim(cotangent, row_index, 0, keepdims=False).astype(jnp.float32)
        weight_sum = weight_sum + jnp.einsum('klc,le->kce', filtered_full, cot_row, precision=precise)
        return (weight_sum, out_row)
    all_rows = jnp.arange(NLAT, dtype=jnp.int32)
    weight_sum, conv_output = lax.scan(forward_step, jnp.zeros((K, C, C), jnp.float32), all_rows)
    weight_grad = weight_sum / jnp.sqrt(jnp.float32(NLAT * NLON))

    def mixed_of(cot_rows):
        mixed = jnp.einsum('ile,kce->kilc', cot_rows.astype(jnp.float32), weights_full, precision=precise)
        return lax.optimization_barrier(mixed.astype(jnp.bfloat16))
    cot_polar = jnp.concatenate([cotangent[:P_SIZE], cotangent[NLAT - P_SIZE:]], axis=0)
    mixed_polar = mixed_of(cot_polar).astype(jnp.float32)

    def pole_terms(pole):
        terms = jnp.zeros((P_SIZE + 2 * R, NLON, C), jnp.float32)
        for offset in range(P_SIZE):
            for lat_tap in range(2 * R + 1):
                kernel_row = cycle_full[:, pole * P_SIZE + offset, lat_tap]
                matrix = kernel_row[:, trans_index]
                contrib = jnp.einsum('kml,klc->mc', matrix, mixed_polar[:, pole * P_SIZE + offset], precision=precise)
                terms = terms.at[offset + lat_tap].add(contrib)
        return terms
    polar_extra = jnp.concatenate([pole_terms(0)[R:], pole_terms(1)[:P_SIZE + R]], axis=0)

    def backward_step(carry_window, row_index):
        fresh = lax.dynamic_slice_in_dim(cot_pad, row_index + 2 * R, 1, 0)
        full_window = jnp.concatenate([carry_window, mixed_of(fresh)], axis=1)
        coeff_rows = lax.dynamic_slice_in_dim(coeff_pad, row_index, 2 * R + 1, 1)
        coeff_sel = jnp.stack([coeff_rows[:, 2 * R - lat_tap, lat_tap] for lat_tap in range(2 * R + 1)], axis=1)
        reversed_rows = full_window[:, ::-1].astype(jnp.float32)
        shifted = jnp.stack([jnp.roll(reversed_rows, H - shift_index, axis=2) for shift_index in range(2 * H + 1)], axis=2)
        total = jnp.einsum('krd,krdlc->lc', coeff_sel, shifted, precision=precise)
        is_top = row_index < P_SIZE + R
        is_bottom = row_index >= NLAT - P_SIZE - R
        picked = jnp.where(is_top, row_index, row_index - (NLAT - P_SIZE - R) + (P_SIZE + R))
        picked = jnp.clip(picked, 0, 2 * (P_SIZE + R) - 1).astype(jnp.int32)
        extra_row = lax.dynamic_index_in_dim(polar_extra, picked, 0, keepdims=False)
        total = total + jnp.where(is_top | is_bottom, extra_row, jnp.zeros_like(extra_row))
        return (full_window[:, 1:], total.astype(jnp.bfloat16))
    first_window = mixed_of(cot_pad[:2 * R])
    last_window, signal_grad = lax.scan(backward_step, first_window, all_rows)
    return (conv_output, signal_grad, weight_grad)
```

```python
import math

import jax
import jax.numpy as jnp
from jax import lax
from jax.sharding import Mesh, PartitionSpec as P

K = 4
R = 1
H = 8
P_SIZE = 2
TAPS = 2 * R + 1
LAGS = 2 * H + 1
SLAB = P_SIZE + R
LON = ("ring", "pair", "core")
CHIPS = ("lat", "ring", "pair")


def dot(spec, a, b):
    return jnp.einsum(spec, a, b, preferred_element_type=jnp.float32)


def bf16(x):
    return x.astype(jnp.bfloat16)


def band_coefficients(band_kernel, support_width, first_row, total_rows, row_count):
    padded_kernel = jnp.pad(band_kernel, ((0, 0), (R, R), (0, 0), (0, 0)))
    padded_width = jnp.pad(support_width, (R, R))
    kernel_rows = lax.dynamic_slice_in_dim(padded_kernel, first_row, row_count, 1)
    width_rows = lax.dynamic_slice_in_dim(padded_width, first_row, row_count, 0)
    global_rows = first_row - R + jnp.arange(row_count, dtype=jnp.int32)
    polar_rows = (global_rows < P_SIZE) | (global_rows >= total_rows - P_SIZE)
    offsets = jnp.abs(jnp.arange(LAGS, dtype=jnp.int32) - H)
    allowed = (offsets[None, :] <= width_rows[:, None]) & jnp.logical_not(polar_rows)[:, None]
    return jnp.where(allowed[None, :, None, :], kernel_rows, jnp.zeros_like(kernel_rows))


def band_matrices(rows, lon_count, forward):
    outputs = jnp.arange(lon_count, dtype=jnp.int32)[:, None, None]
    inputs = jnp.arange(lon_count + 2 * H, dtype=jnp.int32)[None, :, None]
    shifts = jnp.arange(LAGS, dtype=jnp.int32)[None, None, :]
    table = outputs - inputs + 2 * H == shifts if forward else inputs - outputs == shifts
    return bf16(dot("ktrd,amd->tkarm", rows, bf16(table)))


def windows(left, field, right):
    ext = jnp.concatenate([left, field, right], axis=1)
    ext = jnp.pad(ext, ((R, R), (0, 0), (0, 0)))
    return jnp.stack([ext[t : t + field.shape[0]] for t in range(TAPS)], axis=1)


def block_diagonal(a, b):
    upper = jnp.pad(a, ((0, 0), (0, 0), (0, b.shape[2]), (0, 0)))
    lower = jnp.pad(b, ((0, 0), (0, 0), (a.shape[2], 0), (0, 0)))
    return jnp.concatenate([upper, lower], axis=1)


def local(signal, cotangent, weights, band_kernel, cycle_kernel, support_width):
    lat_count, lon_count, channels = signal.shape
    lat_devices = lax.axis_size("lat")
    lon_devices = lax.axis_size(LON)
    lat_index = lax.axis_index("lat")
    lon_index = lax.axis_index(LON)
    core = lax.axis_index("core")
    chip = lon_index // 2
    lon_total = lon_count * lon_devices
    total_rows = lat_count * lat_devices
    first_row = lat_index * lat_count
    is_top = lat_index == 0
    is_polar = is_top | (lat_index == lat_devices - 1)
    swap = [(0, 1), (1, 0)]
    assert lon_count == H

    to_right = [(i, (i + 1) % lon_devices) for i in range(lon_devices)]
    to_left = [(j, i) for i, j in to_right]

    def sector_edges(field):
        return lax.ppermute(field, LON, to_right), lax.ppermute(field, LON, to_left)

    signal_left, signal_right = sector_edges(signal)

    both = jnp.stack([signal, cotangent])
    first, last = both[:, :R], both[:, lat_count - R :]
    if lat_devices == 2:
        edges = lax.ppermute(jnp.where(is_top, last, first), "lat", swap)
    else:
        up = [(i, i + 1) for i in range(lat_devices - 1)]
        down = [(j, i) for i, j in up]
        edges = jnp.concatenate([lax.ppermute(last, "lat", up), lax.ppermute(first, "lat", down)], axis=1)
    count = edges.shape[1]

    cot_left, cot_right = sector_edges(cotangent)
    edges, band_kernel, cycle_kernel, support_width = lax.optimization_barrier(
        (edges, band_kernel, cycle_kernel, support_width)
    )

    slab = jnp.concatenate(
        [
            jnp.where(is_top, signal[:SLAB], signal[lat_count - SLAB :]),
            edges[0],
            jnp.where(is_top, cotangent[:P_SIZE], cotangent[lat_count - P_SIZE :]),
            edges[1],
        ]
    )
    sectors = lon_devices // 2
    even = lax.all_to_all(jnp.broadcast_to(slab[None], (sectors,) + slab.shape), ("ring", "pair"), 0, 0)
    odd = lax.ppermute(even, "core", swap)
    circle = jnp.stack([jnp.where(core == 0, even, odd), jnp.where(core == 0, odd, even)], axis=1)
    circle = circle.reshape((lon_devices,) + slab.shape)
    circle = jnp.moveaxis(circle, 0, 1).reshape(slab.shape[0], lon_total, channels)
    signal_circle, cot_circle = circle[: SLAB + count], circle[SLAB + count :]

    coeffs = band_coefficients(band_kernel, support_width, first_row, total_rows, lat_count + 2 * R)
    forward = band_matrices(coeffs[:, R : R + lat_count], lon_count, True)

    def lag_vector(rows):
        return jnp.concatenate([rows[..., H:], jnp.zeros(rows.shape[:-1] + (lon_total - LAGS,), rows.dtype), rows[..., :H]], -1)

    reads = [coeffs[:, R, 0], coeffs[:, lat_count, 2 * R]]
    gives = [coeffs[:, 0, 2 * R], coeffs[:, lat_count + R, 0]]
    zero = jnp.zeros((K, lon_total), jnp.bfloat16)
    if count == 1:
        edge_forward = lag_vector(jnp.where(is_top, reads[1], reads[0]))[:, None, None]
        edge_adjoint = lag_vector(jnp.where(is_top, gives[1], gives[0]))[:, None, None]
    else:
        edge_forward = block_diagonal(lag_vector(reads[0])[:, None, None], lag_vector(reads[1])[:, None, None])
        edge_adjoint = block_diagonal(lag_vector(gives[0])[:, None, None], lag_vector(gives[1])[:, None, None])
    top_rows = [[cycle_kernel[:, p, s - p + R] if 0 <= s - p + R < TAPS else zero for s in range(SLAB)] for p in range(P_SIZE)]
    low_rows = [[cycle_kernel[:, P_SIZE + p, s - p] if 0 <= s - p < TAPS else zero for s in range(SLAB)] for p in range(P_SIZE)]
    slab_kernel = jnp.where(
        is_top,
        jnp.stack([jnp.stack(row, axis=1) for row in top_rows], axis=1),
        jnp.stack([jnp.stack(row, axis=1) for row in low_rows], axis=1),
    )
    slab_kernel = jnp.where(is_polar, slab_kernel, jnp.zeros_like(slab_kernel))
    lags = jnp.arange(lon_total, dtype=jnp.int32)[:, None, None]
    own_lons = lon_index * lon_count + jnp.arange(lon_count, dtype=jnp.int32)
    chip_lons = chip * 2 * lon_count + jnp.arange(2 * lon_count, dtype=jnp.int32)
    all_lons = jnp.arange(lon_total, dtype=jnp.int32)
    distance = (chip_lons[:, None] - all_lons[None, :]) % lon_total
    opposite = (all_lons[None, :] - own_lons[:, None]) % lon_total
    forward_cycle = bf16(dot("kpsd,dam->kpasm", block_diagonal(slab_kernel, edge_forward), bf16(distance[None] == lags)))
    adjoint_kernel = block_diagonal(jnp.swapaxes(slab_kernel, 1, 2), edge_adjoint)

    def placed(extra, polar_count):
        polar, edge = extra[:, :polar_count], extra[:, polar_count:]

        def rows(block, before):
            return jnp.pad(block, ((0, 0), (before, lat_count - block.shape[1] - before), (0, 0), (0, 0)))

        if count == 1:
            return jnp.where(
                is_top,
                rows(polar, 0) + rows(edge, lat_count - R),
                rows(polar, lat_count - polar_count) + rows(edge, 0),
            )
        out = jnp.where(is_top, rows(polar, 0), rows(polar, lat_count - polar_count))
        return out + rows(edge[:, :R], 0) + rows(edge[:, R:], lat_count - R)

    left, right, _, _ = lax.optimization_barrier((signal_left, signal_right, cot_left, cot_right))
    banded = dot("ikarm,irmc->ikac", forward, windows(left, signal, right))
    banded = jnp.moveaxis(banded, 1, 0)
    scale = 1.0 / math.sqrt(total_rows * lon_total)
    partial = (dot("kiac,iae->kce", bf16(banded), cotangent) * scale).reshape(2, -1, channels)
    given = bf16(jnp.where(core == 0, partial[1], partial[0]))
    kept = jnp.where(core == 0, partial[0], partial[1])
    kept = kept + lax.ppermute(given, "core", swap).astype(jnp.float32)

    extra = dot("kpasm,smc->kpac", forward_cycle, signal_circle)
    partner = jnp.where(core == 0, cot_right, cot_left)
    chip_rows = jnp.concatenate([jnp.where(core == 0, cotangent, partner), jnp.where(core == 0, partner, cotangent)], axis=1)
    polar_rows = jnp.where(is_top, chip_rows[:P_SIZE], chip_rows[lat_count - P_SIZE :])
    if count == 1:
        edge_rows = jnp.where(is_top, chip_rows[lat_count - R :], chip_rows[:R])
    else:
        edge_rows = jnp.concatenate([chip_rows[:R], chip_rows[lat_count - R :]])
    kept_extra = lax.dynamic_slice_in_dim(bf16(extra), core * (K // 2), K // 2, 0)
    extra_partial = dot("kpac,pae->kce", kept_extra, jnp.concatenate([polar_rows, edge_rows]))
    kept = kept + (extra_partial * scale).reshape(-1, channels)

    group = lat_devices * lon_devices // 2
    parts = lax.all_to_all(bf16(kept).reshape(group, -1, channels), CHIPS, 0, 0)
    chunk = bf16(jnp.sum(parts.astype(jnp.float32), axis=0))
    half = lax.all_to_all(jnp.broadcast_to(chunk[None], (group,) + chunk.shape), CHIPS, 0, 0)
    other = lax.ppermute(half, "core", swap)
    weight_grad = jnp.stack([jnp.where(core == 0, half, other), jnp.where(core == 0, other, half)])
    weight_grad = weight_grad.reshape(K, channels, channels).astype(jnp.float32)

    coeffs, adjoint_kernel, extra, kept = lax.optimization_barrier((coeffs, adjoint_kernel, extra, kept))
    own_extra = lax.dynamic_slice_in_dim(extra, core * lon_count, lon_count, 2)
    filtered = bf16(banded + placed(own_extra, P_SIZE))
    conv_output = bf16(dot("kiac,kce->iae", filtered, weights))

    adjoint_rows = jnp.stack([coeffs[:, t : t + lat_count, 2 * R - t] for t in range(TAPS)], axis=2)
    adjoint = band_matrices(adjoint_rows, lon_count, False)
    adjoint_cycle = bf16(dot("kspd,dbm->ksbpm", adjoint_kernel, bf16(opposite[None] == lags)))
    spread = dot("ikarm,irme->ikae", adjoint, windows(cot_left, cotangent, cot_right))
    spread = jnp.moveaxis(spread, 1, 0)
    spread = spread + placed(dot("ksbpm,pme->ksbe", adjoint_cycle, cot_circle), SLAB)
    signal_grad = bf16(dot("kjbe,kce->jbc", bf16(spread), weights))
    return conv_output, signal_grad, weight_grad


def solution(mesh):
    lat_devices, lon_devices = mesh.devices.shape
    split = Mesh(mesh.devices.reshape(lat_devices, lon_devices // 4, 2, 2), ("lat",) + LON)
    placed = (P("lat", LON, None), P("lat", LON, None), P(), P(), P(), P())
    return jax.shard_map(
        local,
        mesh=split,
        in_specs=placed,
        out_specs=(P("lat", LON, None), P("lat", LON, None), P()),
        check_vma=False,
    )
```

```python
import math

import jax
import jax.numpy as jnp
from jax import lax
from jax.sharding import Mesh, PartitionSpec as P

K = 4
R = 1
H = 8
P_SIZE = 2
TAPS = 2 * R + 1
LAGS = 2 * H + 1
SLAB = P_SIZE + R
LON = ("ring", "pair", "core")
CHIPS = ("lat", "ring", "pair")


def dot(spec, a, b):
    return jnp.einsum(spec, a, b, preferred_element_type=jnp.float32)


def bf16(x):
    return x.astype(jnp.bfloat16)


def band_coefficients(band_kernel, support_width, first_row, total_rows, row_count):
    padded_kernel = jnp.pad(band_kernel, ((0, 0), (R, R), (0, 0), (0, 0)))
    padded_width = jnp.pad(support_width, (R, R))
    kernel_rows = lax.dynamic_slice_in_dim(padded_kernel, first_row, row_count, 1)
    width_rows = lax.dynamic_slice_in_dim(padded_width, first_row, row_count, 0)
    global_rows = first_row - R + jnp.arange(row_count, dtype=jnp.int32)
    polar_rows = (global_rows < P_SIZE) | (global_rows >= total_rows - P_SIZE)
    offsets = jnp.abs(jnp.arange(LAGS, dtype=jnp.int32) - H)
    allowed = (offsets[None, :] <= width_rows[:, None]) & jnp.logical_not(polar_rows)[:, None]
    return jnp.where(allowed[None, :, None, :], kernel_rows, jnp.zeros_like(kernel_rows))


def band_matrices(rows, lon_count, forward):
    outputs = jnp.arange(lon_count, dtype=jnp.int32)[:, None, None]
    inputs = jnp.arange(lon_count + 2 * H, dtype=jnp.int32)[None, :, None]
    shifts = jnp.arange(LAGS, dtype=jnp.int32)[None, None, :]
    table = outputs - inputs + 2 * H == shifts if forward else inputs - outputs == shifts
    return bf16(dot("ktrd,amd->tkarm", rows, bf16(table)))


def windows(left, field, right):
    ext = jnp.concatenate([left, field, right], axis=1)
    ext = jnp.pad(ext, ((R, R), (0, 0), (0, 0)))
    return jnp.stack([ext[t : t + field.shape[0]] for t in range(TAPS)], axis=1)


def block_diagonal(a, b):
    upper = jnp.pad(a, ((0, 0), (0, 0), (0, b.shape[2]), (0, 0)))
    lower = jnp.pad(b, ((0, 0), (0, 0), (a.shape[2], 0), (0, 0)))
    return jnp.concatenate([upper, lower], axis=1)


def local(signal, cotangent, weights, band_kernel, cycle_kernel, support_width):
    lat_count, lon_count, channels = signal.shape
    lat_devices = lax.axis_size("lat")
    lon_devices = lax.axis_size(LON)
    lat_index = lax.axis_index("lat")
    lon_index = lax.axis_index(LON)
    core = lax.axis_index("core")
    chip = lon_index // 2
    lon_total = lon_count * lon_devices
    total_rows = lat_count * lat_devices
    first_row = lat_index * lat_count
    is_top = lat_index == 0
    is_bottom = lat_index == lat_devices - 1
    is_polar = is_top | is_bottom
    swap = [(0, 1), (1, 0)]
    assert lon_count == H

    to_right = [(i, (i + 1) % lon_devices) for i in range(lon_devices)]
    to_left = [(j, i) for i, j in to_right]

    def sector_edges(field):
        return lax.ppermute(field, LON, to_right), lax.ppermute(field, LON, to_left)

    def polar_slab(field, height):
        return lax.dynamic_slice_in_dim(field, jnp.where(is_top, 0, lat_count - height), height, 0)

    signal_left, signal_right = sector_edges(signal)

    polar_rows = jnp.concatenate([polar_slab(signal, SLAB), polar_slab(cotangent, P_SIZE)])
    fill = jnp.zeros((SLAB + P_SIZE - 2 * R, lon_count, channels), signal.dtype)
    first = jnp.concatenate([signal[:R], cotangent[:R], fill])
    last = jnp.concatenate([signal[lat_count - R :], cotangent[lat_count - R :], fill])
    target = jnp.arange(lat_devices, dtype=jnp.int32)[:, None, None, None]
    chunks = jnp.where(target == lat_index, polar_rows[None], jnp.where(target > lat_index, last[None], first[None]))
    sectors = lon_devices // 2
    sent = jnp.broadcast_to(chunks[:, None], (lat_devices, sectors) + polar_rows.shape)
    got = lax.all_to_all(sent.reshape((-1,) + polar_rows.shape), CHIPS, 0, 0).reshape(sent.shape)

    def from_band(band):
        return lax.dynamic_index_in_dim(got, band, 0, keepdims=False)

    polar_got = from_band(lat_index)
    if lat_devices == 2:
        edges = [from_band(1 - lat_index)]
    else:
        zero_edge = jnp.zeros_like(polar_got)
        edges = [
            jnp.where(is_top, zero_edge, from_band(jnp.maximum(lat_index - 1, 0))),
            jnp.where(is_bottom, zero_edge, from_band(jnp.minimum(lat_index + 1, lat_devices - 1))),
        ]
    count = len(edges)
    if count == 1:
        facing = jnp.where(is_top, cotangent[lat_count - R :], cotangent[:R])
    else:
        facing = jnp.concatenate([cotangent[:R], cotangent[lat_count - R :]])
    even = jnp.concatenate(
        [polar_got[:, :SLAB]] + [e[:, :R] for e in edges] + [polar_got[:, SLAB:]] + [e[:, R : 2 * R] for e in edges], axis=1
    )
    rows = even.shape[1]
    swapped = lax.ppermute(jnp.concatenate([even.reshape((-1,) + even.shape[2:]), facing]), "core", swap)
    odd = swapped[: sectors * rows].reshape(even.shape)
    partner_facing = swapped[sectors * rows :]
    circle = jnp.stack([jnp.where(core == 0, even, odd), jnp.where(core == 0, odd, even)], axis=1)
    circle = circle.reshape((lon_devices,) + even.shape[1:])
    circle = jnp.moveaxis(circle, 0, 1).reshape(rows, lon_total, channels)
    signal_circle, cot_circle = circle[: SLAB + count], circle[SLAB + count :]

    signal_left, signal_right, band_kernel, cycle_kernel, support_width, _ = lax.optimization_barrier(
        (signal_left, signal_right, band_kernel, cycle_kernel, support_width, sent)
    )
    coeffs = band_coefficients(band_kernel, support_width, first_row, total_rows, lat_count + 2 * R)
    forward = band_matrices(coeffs[:, R : R + lat_count], lon_count, True)

    def lag_vector(rows):
        return jnp.concatenate([rows[..., H:], jnp.zeros(rows.shape[:-1] + (lon_total - LAGS,), rows.dtype), rows[..., :H]], -1)

    reads = [coeffs[:, R, 0], coeffs[:, lat_count, 2 * R]]
    gives = [coeffs[:, 0, 2 * R], coeffs[:, lat_count + R, 0]]
    zero = jnp.zeros((K, lon_total), jnp.bfloat16)
    if count == 1:
        edge_forward = lag_vector(jnp.where(is_top, reads[1], reads[0]))[:, None, None]
        edge_adjoint = lag_vector(jnp.where(is_top, gives[1], gives[0]))[:, None, None]
    else:
        edge_forward = block_diagonal(lag_vector(reads[0])[:, None, None], lag_vector(reads[1])[:, None, None])
        edge_adjoint = block_diagonal(lag_vector(gives[0])[:, None, None], lag_vector(gives[1])[:, None, None])
    top_rows = [[cycle_kernel[:, p, s - p + R] if 0 <= s - p + R < TAPS else zero for s in range(SLAB)] for p in range(P_SIZE)]
    low_rows = [[cycle_kernel[:, P_SIZE + p, s - p] if 0 <= s - p < TAPS else zero for s in range(SLAB)] for p in range(P_SIZE)]
    slab_kernel = jnp.where(
        is_top,
        jnp.stack([jnp.stack(row, axis=1) for row in top_rows], axis=1),
        jnp.stack([jnp.stack(row, axis=1) for row in low_rows], axis=1),
    )
    slab_kernel = jnp.where(is_polar, slab_kernel, jnp.zeros_like(slab_kernel))
    lags = jnp.arange(lon_total, dtype=jnp.int32)[:, None, None]
    own_lons = lon_index * lon_count + jnp.arange(lon_count, dtype=jnp.int32)
    chip_lons = chip * 2 * lon_count + jnp.arange(2 * lon_count, dtype=jnp.int32)
    all_lons = jnp.arange(lon_total, dtype=jnp.int32)
    distance = (chip_lons[:, None] - all_lons[None, :]) % lon_total
    opposite = (all_lons[None, :] - own_lons[:, None]) % lon_total
    forward_cycle = bf16(dot("kpsd,dam->kpasm", block_diagonal(slab_kernel, edge_forward), bf16(distance[None] == lags)))
    adjoint_kernel = block_diagonal(jnp.swapaxes(slab_kernel, 1, 2), edge_adjoint)

    def placed(extra, polar_count):
        polar, edge = extra[:, :polar_count], extra[:, polar_count:]

        def rows(block, before):
            return jnp.pad(block, ((0, 0), (before, lat_count - block.shape[1] - before), (0, 0), (0, 0)))

        if count == 1:
            return jnp.where(
                is_top,
                rows(polar, 0) + rows(edge, lat_count - R),
                rows(polar, lat_count - polar_count) + rows(edge, 0),
            )
        out = jnp.where(is_top, rows(polar, 0), rows(polar, lat_count - polar_count))
        return out + rows(edge[:, :R], 0) + rows(edge[:, R:], lat_count - R)

    banded = dot("ikarm,irmc->ikac", forward, windows(signal_left, signal, signal_right))
    banded = jnp.moveaxis(banded, 1, 0)
    scale = 1.0 / math.sqrt(total_rows * lon_total)
    partial = (dot("kiac,iae->kce", bf16(banded), cotangent) * scale).reshape(2, -1, channels)
    given = bf16(jnp.where(core == 0, partial[1], partial[0]))
    kept = jnp.where(core == 0, partial[0], partial[1])
    given, late = lax.optimization_barrier((given, cotangent))
    cot_left, cot_right = sector_edges(late)
    kept = kept + lax.ppermute(given, "core", swap).astype(jnp.float32)

    extra = dot("kpasm,smc->kpac", forward_cycle, signal_circle)
    chip_polar = lax.dynamic_slice_in_dim(cot_circle[:P_SIZE], chip * 2 * lon_count, 2 * lon_count, 1)
    facing_pair = [jnp.where(core == 0, facing, partner_facing), jnp.where(core == 0, partner_facing, facing)]
    chip_facing = jnp.concatenate(facing_pair, axis=1)
    kept_extra = lax.dynamic_slice_in_dim(bf16(extra), core * (K // 2), K // 2, 0)
    extra_partial = dot("kpac,pae->kce", kept_extra, jnp.concatenate([chip_polar, chip_facing]))
    kept = kept + (extra_partial * scale).reshape(-1, channels)

    group = lat_devices * lon_devices // 2
    parts = lax.all_to_all(bf16(kept).reshape(group, -1, channels), CHIPS, 0, 0)
    chunk = bf16(jnp.sum(parts.astype(jnp.float32), axis=0))
    half = lax.all_to_all(jnp.broadcast_to(chunk[None], (group,) + chunk.shape), CHIPS, 0, 0)
    coeffs, adjoint_kernel, extra, kept = lax.optimization_barrier((coeffs, adjoint_kernel, extra, kept))
    own_extra = lax.dynamic_slice_in_dim(extra, core * lon_count, lon_count, 2)
    filtered = bf16(banded + placed(own_extra, P_SIZE))
    conv_output = bf16(dot("kiac,kce->iae", filtered, weights))

    adjoint_rows = jnp.stack([coeffs[:, t : t + lat_count, 2 * R - t] for t in range(TAPS)], axis=2)
    adjoint = band_matrices(adjoint_rows, lon_count, False)
    adjoint_cycle = bf16(dot("kspd,dbm->ksbpm", adjoint_kernel, bf16(opposite[None] == lags)))
    cot_left, cot_right, _ = lax.optimization_barrier((cot_left, cot_right, chunk))
    spread = dot("ikarm,irme->ikae", adjoint, windows(cot_left, cotangent, cot_right))
    spread = jnp.moveaxis(spread, 1, 0)
    spread = spread + placed(dot("ksbpm,pme->ksbe", adjoint_cycle, cot_circle), SLAB)
    signal_grad = bf16(dot("kjbe,kce->jbc", bf16(spread), weights))
    half, conv_output, signal_grad = lax.optimization_barrier((half, conv_output, signal_grad))
    other = lax.ppermute(half, "core", swap)
    weight_grad = jnp.stack([jnp.where(core == 0, half, other), jnp.where(core == 0, other, half)])
    weight_grad = weight_grad.reshape(K, channels, channels).astype(jnp.float32)
    return conv_output, signal_grad, weight_grad


def solution(mesh):
    lat_devices, lon_devices = mesh.devices.shape
    split = Mesh(mesh.devices.reshape(lat_devices, lon_devices // 4, 2, 2), ("lat",) + LON)
    placed = (P("lat", LON, None), P("lat", LON, None), P(), P(), P(), P())
    return jax.shard_map(
        local,
        mesh=split,
        in_specs=placed,
        out_specs=(P("lat", LON, None), P("lat", LON, None), P()),
        check_vma=False,
    )
```

```python
import math

import jax
import jax.numpy as jnp
from jax import lax
from jax.sharding import Mesh, PartitionSpec as P

K = 4
R = 1
H = 8
P_SIZE = 2
TAPS = 2 * R + 1
LAGS = 2 * H + 1
SLAB = P_SIZE + R
LON = ("ring", "pair", "core")
CHIPS = ("lat", "ring", "pair")


def dot(spec, a, b):
    return jnp.einsum(spec, a, b, preferred_element_type=jnp.float32)


def bf16(x):
    return x.astype(jnp.bfloat16)


def band_coefficients(band_kernel, support_width, first_row, total_rows, row_count):
    padded_kernel = jnp.pad(band_kernel, ((0, 0), (R, R), (0, 0), (0, 0)))
    padded_width = jnp.pad(support_width, (R, R))
    kernel_rows = lax.dynamic_slice_in_dim(padded_kernel, first_row, row_count, 1)
    width_rows = lax.dynamic_slice_in_dim(padded_width, first_row, row_count, 0)
    global_rows = first_row - R + jnp.arange(row_count, dtype=jnp.int32)
    polar_rows = (global_rows < P_SIZE) | (global_rows >= total_rows - P_SIZE)
    offsets = jnp.abs(jnp.arange(LAGS, dtype=jnp.int32) - H)
    allowed = (offsets[None, :] <= width_rows[:, None]) & jnp.logical_not(polar_rows)[:, None]
    return jnp.where(allowed[None, :, None, :], kernel_rows, jnp.zeros_like(kernel_rows))


def band_matrices(rows, lon_count, forward):
    outputs = jnp.arange(lon_count, dtype=jnp.int32)[:, None, None]
    inputs = jnp.arange(lon_count + 2 * H, dtype=jnp.int32)[None, :, None]
    shifts = jnp.arange(LAGS, dtype=jnp.int32)[None, None, :]
    table = outputs - inputs + 2 * H == shifts if forward else inputs - outputs == shifts
    return bf16(dot("ktrd,amd->tkarm", rows, bf16(table)))


def windows(left, field, right):
    ext = jnp.concatenate([left, field, right], axis=1)
    ext = jnp.pad(ext, ((R, R), (0, 0), (0, 0)))
    return jnp.stack([ext[t : t + field.shape[0]] for t in range(TAPS)], axis=1)


def block_diagonal(a, b):
    upper = jnp.pad(a, ((0, 0), (0, 0), (0, b.shape[2]), (0, 0)))
    lower = jnp.pad(b, ((0, 0), (0, 0), (a.shape[2], 0), (0, 0)))
    return jnp.concatenate([upper, lower], axis=1)


def local(signal, cotangent, weights, band_kernel, cycle_kernel, support_width):
    lat_count, lon_count, channels = signal.shape
    lat_devices = lax.axis_size("lat")
    lon_devices = lax.axis_size(LON)
    lat_index = lax.axis_index("lat")
    lon_index = lax.axis_index(LON)
    core = lax.axis_index("core")
    chip = lon_index // 2
    lon_total = lon_count * lon_devices
    total_rows = lat_count * lat_devices
    first_row = lat_index * lat_count
    is_top = lat_index == 0
    is_bottom = lat_index == lat_devices - 1
    is_polar = is_top | is_bottom
    swap = [(0, 1), (1, 0)]
    assert lon_count == H

    to_right = [(i, (i + 1) % lon_devices) for i in range(lon_devices)]
    to_left = [(j, i) for i, j in to_right]

    def sector_edges(field):
        return lax.ppermute(field, LON, to_right), lax.ppermute(field, LON, to_left)

    def polar_slab(field, height):
        return lax.dynamic_slice_in_dim(field, jnp.where(is_top, 0, lat_count - height), height, 0)

    signal_left, signal_right = sector_edges(signal)
    both = lax.optimization_barrier(jnp.stack([signal, cotangent]))

    polar_rows = jnp.concatenate([polar_slab(both[0], SLAB), polar_slab(both[1], P_SIZE)])
    fill = jnp.zeros((SLAB + P_SIZE - 2 * R, lon_count, channels), signal.dtype)
    first = jnp.concatenate([both[0, :R], both[1, :R], fill])
    last = jnp.concatenate([both[0, lat_count - R :], both[1, lat_count - R :], fill])
    target = jnp.arange(lat_devices, dtype=jnp.int32)[:, None, None, None]
    chunks = jnp.where(target == lat_index, polar_rows[None], jnp.where(target > lat_index, last[None], first[None]))
    sectors = lon_devices // 2
    sent = jnp.broadcast_to(chunks[:, None], (lat_devices, sectors) + polar_rows.shape)
    got = lax.all_to_all(sent.reshape((-1,) + polar_rows.shape), CHIPS, 0, 0).reshape(sent.shape)

    def from_band(band):
        return lax.dynamic_index_in_dim(got, band, 0, keepdims=False)

    polar_got = from_band(lat_index)
    if lat_devices == 2:
        edges = [from_band(1 - lat_index)]
    else:
        zero_edge = jnp.zeros_like(polar_got)
        edges = [
            jnp.where(is_top, zero_edge, from_band(jnp.maximum(lat_index - 1, 0))),
            jnp.where(is_bottom, zero_edge, from_band(jnp.minimum(lat_index + 1, lat_devices - 1))),
        ]
    count = len(edges)
    if count == 1:
        facing = jnp.where(is_top, both[1, lat_count - R :], both[1, :R])
    else:
        facing = jnp.concatenate([both[1, :R], both[1, lat_count - R :]])
    even = jnp.concatenate(
        [polar_got[:, :SLAB]] + [e[:, :R] for e in edges] + [polar_got[:, SLAB:]] + [e[:, R : 2 * R] for e in edges], axis=1
    )
    rows = even.shape[1]
    swapped = lax.ppermute(jnp.concatenate([even.reshape((-1,) + even.shape[2:]), facing]), "core", swap)
    odd = swapped[: sectors * rows].reshape(even.shape)
    partner_facing = swapped[sectors * rows :]
    circle = jnp.stack([jnp.where(core == 0, even, odd), jnp.where(core == 0, odd, even)], axis=1)
    circle = circle.reshape((lon_devices,) + even.shape[1:])
    circle = jnp.moveaxis(circle, 0, 1).reshape(rows, lon_total, channels)
    signal_circle, cot_circle = circle[: SLAB + count], circle[SLAB + count :]

    band_kernel, cycle_kernel, support_width, _ = lax.optimization_barrier(
        (band_kernel, cycle_kernel, support_width, sent)
    )
    coeffs = band_coefficients(band_kernel, support_width, first_row, total_rows, lat_count + 2 * R)
    forward = band_matrices(coeffs[:, R : R + lat_count], lon_count, True)

    def lag_vector(rows):
        return jnp.concatenate([rows[..., H:], jnp.zeros(rows.shape[:-1] + (lon_total - LAGS,), rows.dtype), rows[..., :H]], -1)

    reads = [coeffs[:, R, 0], coeffs[:, lat_count, 2 * R]]
    gives = [coeffs[:, 0, 2 * R], coeffs[:, lat_count + R, 0]]
    zero = jnp.zeros((K, lon_total), jnp.bfloat16)
    if count == 1:
        edge_forward = lag_vector(jnp.where(is_top, reads[1], reads[0]))[:, None, None]
        edge_adjoint = lag_vector(jnp.where(is_top, gives[1], gives[0]))[:, None, None]
    else:
        edge_forward = block_diagonal(lag_vector(reads[0])[:, None, None], lag_vector(reads[1])[:, None, None])
        edge_adjoint = block_diagonal(lag_vector(gives[0])[:, None, None], lag_vector(gives[1])[:, None, None])
    top_rows = [[cycle_kernel[:, p, s - p + R] if 0 <= s - p + R < TAPS else zero for s in range(SLAB)] for p in range(P_SIZE)]
    low_rows = [[cycle_kernel[:, P_SIZE + p, s - p] if 0 <= s - p < TAPS else zero for s in range(SLAB)] for p in range(P_SIZE)]
    slab_kernel = jnp.where(
        is_top,
        jnp.stack([jnp.stack(row, axis=1) for row in top_rows], axis=1),
        jnp.stack([jnp.stack(row, axis=1) for row in low_rows], axis=1),
    )
    slab_kernel = jnp.where(is_polar, slab_kernel, jnp.zeros_like(slab_kernel))
    def placed(extra, polar_count):
        polar, edge = extra[:, :polar_count], extra[:, polar_count:]

        def rows(block, before):
            return jnp.pad(block, ((0, 0), (before, lat_count - block.shape[1] - before), (0, 0), (0, 0)))

        if count == 1:
            return jnp.where(
                is_top,
                rows(polar, 0) + rows(edge, lat_count - R),
                rows(polar, lat_count - polar_count) + rows(edge, 0),
            )
        out = jnp.where(is_top, rows(polar, 0), rows(polar, lat_count - polar_count))
        return out + rows(edge[:, :R], 0) + rows(edge[:, R:], lat_count - R)

    banded = dot("ikarm,irmc->ikac", forward, windows(signal_left, signal, signal_right))
    banded = bf16(jnp.moveaxis(banded, 1, 0))
    scale = 1.0 / math.sqrt(total_rows * lon_total)
    partial = (dot("kiac,iae->kce", banded, cotangent) * scale).reshape(2, -1, channels)
    given = bf16(jnp.where(core == 0, partial[1], partial[0]))
    kept = jnp.where(core == 0, partial[0], partial[1])
    kept = kept + lax.ppermute(given, "core", swap).astype(jnp.float32)

    slab_kernel, edge_forward, edge_adjoint, _ = lax.optimization_barrier((slab_kernel, edge_forward, edge_adjoint, given))
    lags = jnp.arange(lon_total, dtype=jnp.int32)[:, None, None]
    own_lons = lon_index * lon_count + jnp.arange(lon_count, dtype=jnp.int32)
    chip_lons = chip * 2 * lon_count + jnp.arange(2 * lon_count, dtype=jnp.int32)
    all_lons = jnp.arange(lon_total, dtype=jnp.int32)
    distance = (chip_lons[:, None] - all_lons[None, :]) % lon_total
    opposite = (all_lons[None, :] - own_lons[:, None]) % lon_total
    forward_cycle = bf16(dot("kpsd,dam->kpasm", block_diagonal(slab_kernel, edge_forward), bf16(distance[None] == lags)))
    adjoint_kernel = block_diagonal(jnp.swapaxes(slab_kernel, 1, 2), edge_adjoint)


    extra = dot("kpasm,smc->kpac", forward_cycle, signal_circle)
    chip_polar = lax.dynamic_slice_in_dim(cot_circle[:P_SIZE], chip * 2 * lon_count, 2 * lon_count, 1)
    facing_pair = [jnp.where(core == 0, facing, partner_facing), jnp.where(core == 0, partner_facing, facing)]
    chip_facing = jnp.concatenate(facing_pair, axis=1)
    kept_extra = lax.dynamic_slice_in_dim(bf16(extra), core * (K // 2), K // 2, 0)
    extra_partial = dot("kpac,pae->kce", kept_extra, jnp.concatenate([chip_polar, chip_facing]))
    kept = kept + (extra_partial * scale).reshape(-1, channels)

    group = lat_devices * lon_devices // 2
    parts = lax.all_to_all(bf16(kept).reshape(group, -1, channels), CHIPS, 0, 0)
    chunk = bf16(jnp.sum(parts.astype(jnp.float32), axis=0))
    half = lax.all_to_all(jnp.broadcast_to(chunk[None], (group,) + chunk.shape), CHIPS, 0, 0)
    coeffs, adjoint_kernel, extra, late, kept = lax.optimization_barrier((coeffs, adjoint_kernel, extra, cotangent, kept))
    cot_left, cot_right = sector_edges(late)
    own_extra = lax.dynamic_slice_in_dim(extra, core * lon_count, lon_count, 2)
    filtered = bf16(banded + placed(own_extra, P_SIZE))
    conv_output = bf16(dot("kiac,kce->iae", filtered, weights))

    adjoint_rows = jnp.stack([coeffs[:, t : t + lat_count, 2 * R - t] for t in range(TAPS)], axis=2)
    adjoint = band_matrices(adjoint_rows, lon_count, False)
    adjoint_cycle = bf16(dot("kspd,dbm->ksbpm", adjoint_kernel, bf16(opposite[None] == lags)))
    spread = dot("ikarm,irme->ikae", adjoint, windows(cot_left, cotangent, cot_right))
    spread = jnp.moveaxis(spread, 1, 0)
    spread = spread + placed(dot("ksbpm,pme->ksbe", adjoint_cycle, cot_circle), SLAB)
    signal_grad = bf16(dot("kjbe,kce->jbc", bf16(spread), weights))
    half, conv_output, signal_grad = lax.optimization_barrier((half, conv_output, signal_grad))
    other = lax.ppermute(half, "core", swap)
    weight_grad = jnp.stack([jnp.where(core == 0, half, other), jnp.where(core == 0, other, half)])
    weight_grad = weight_grad.reshape(K, channels, channels).astype(jnp.float32)
    return conv_output, signal_grad, weight_grad


def solution(mesh):
    lat_devices, lon_devices = mesh.devices.shape
    split = Mesh(mesh.devices.reshape(lat_devices, lon_devices // 4, 2, 2), ("lat",) + LON)
    placed = (P("lat", LON, None), P("lat", LON, None), P(), P(), P(), P())
    return jax.shard_map(
        local,
        mesh=split,
        in_specs=placed,
        out_specs=(P("lat", LON, None), P("lat", LON, None), P()),
        check_vma=False,
    )
```

```python
import math

import jax
import jax.numpy as jnp
from jax import lax
from jax.sharding import Mesh, PartitionSpec as P

K = 4
R = 1
H = 8
P_SIZE = 2
TAPS = 2 * R + 1
LAGS = 2 * H + 1
SLAB = P_SIZE + R
LON = ("ring", "pair", "core")
CHIPS = ("lat", "ring", "pair")


def dot(spec, a, b):
    return jnp.einsum(spec, a, b, preferred_element_type=jnp.float32)


def bf16(x):
    return x.astype(jnp.bfloat16)


def band_coefficients(band_kernel, support_width, first_row, total_rows, row_count):
    padded_kernel = jnp.pad(band_kernel, ((0, 0), (R, R), (0, 0), (0, 0)))
    padded_width = jnp.pad(support_width, (R, R))
    kernel_rows = lax.dynamic_slice_in_dim(padded_kernel, first_row, row_count, 1)
    width_rows = lax.dynamic_slice_in_dim(padded_width, first_row, row_count, 0)
    global_rows = first_row - R + jnp.arange(row_count, dtype=jnp.int32)
    polar_rows = (global_rows < P_SIZE) | (global_rows >= total_rows - P_SIZE)
    offsets = jnp.abs(jnp.arange(LAGS, dtype=jnp.int32) - H)
    allowed = (offsets[None, :] <= width_rows[:, None]) & jnp.logical_not(polar_rows)[:, None]
    return jnp.where(allowed[None, :, None, :], kernel_rows, jnp.zeros_like(kernel_rows))


def band_matrices(rows, lon_count, forward):
    outputs = jnp.arange(lon_count, dtype=jnp.int32)[:, None, None]
    inputs = jnp.arange(lon_count + 2 * H, dtype=jnp.int32)[None, :, None]
    shifts = jnp.arange(LAGS, dtype=jnp.int32)[None, None, :]
    table = outputs - inputs + 2 * H == shifts if forward else inputs - outputs == shifts
    return bf16(dot("ktrd,amd->tkarm", rows, bf16(table)))


def windows(left, field, right):
    ext = jnp.concatenate([left, field, right], axis=1)
    ext = jnp.pad(ext, ((R, R), (0, 0), (0, 0)))
    return jnp.stack([ext[t : t + field.shape[0]] for t in range(TAPS)], axis=1)


def block_diagonal(a, b):
    upper = jnp.pad(a, ((0, 0), (0, 0), (0, b.shape[2]), (0, 0)))
    lower = jnp.pad(b, ((0, 0), (0, 0), (a.shape[2], 0), (0, 0)))
    return jnp.concatenate([upper, lower], axis=1)


def local(signal, cotangent, weights, band_kernel, cycle_kernel, support_width):
    lat_count, lon_count, channels = signal.shape
    lat_devices = lax.axis_size("lat")
    lon_devices = lax.axis_size(LON)
    lat_index = lax.axis_index("lat")
    lon_index = lax.axis_index(LON)
    core = lax.axis_index("core")
    chip = lon_index // 2
    lon_total = lon_count * lon_devices
    total_rows = lat_count * lat_devices
    first_row = lat_index * lat_count
    is_top = lat_index == 0
    is_bottom = lat_index == lat_devices - 1
    is_polar = is_top | is_bottom
    swap = [(0, 1), (1, 0)]
    assert lon_count == H

    to_right = [(i, (i + 1) % lon_devices) for i in range(lon_devices)]
    to_left = [(j, i) for i, j in to_right]

    def sector_edges(field):
        return lax.ppermute(field, LON, to_right), lax.ppermute(field, LON, to_left)

    def polar_slab(field, height):
        return lax.dynamic_slice_in_dim(field, jnp.where(is_top, 0, lat_count - height), height, 0)

    signal_left, signal_right = sector_edges(signal)
    both = lax.optimization_barrier(jnp.stack([signal, cotangent]))

    polar_rows = jnp.concatenate([polar_slab(both[0], SLAB), polar_slab(both[1], P_SIZE)])
    fill = jnp.zeros((SLAB + P_SIZE - 2 * R, lon_count, channels), signal.dtype)
    first = jnp.concatenate([both[0, :R], both[1, :R], fill])
    last = jnp.concatenate([both[0, lat_count - R :], both[1, lat_count - R :], fill])
    target = jnp.arange(lat_devices, dtype=jnp.int32)[:, None, None, None]
    chunks = jnp.where(target == lat_index, polar_rows[None], jnp.where(target > lat_index, last[None], first[None]))
    sectors = lon_devices // 2
    sent = jnp.broadcast_to(chunks[:, None], (lat_devices, sectors) + polar_rows.shape)
    got = lax.all_to_all(sent.reshape((-1,) + polar_rows.shape), CHIPS, 0, 0).reshape(sent.shape)

    def from_band(band):
        return lax.dynamic_index_in_dim(got, band, 0, keepdims=False)

    polar_got = from_band(lat_index)
    if lat_devices == 2:
        edges = [from_band(1 - lat_index)]
    else:
        zero_edge = jnp.zeros_like(polar_got)
        edges = [
            jnp.where(is_top, zero_edge, from_band(jnp.maximum(lat_index - 1, 0))),
            jnp.where(is_bottom, zero_edge, from_band(jnp.minimum(lat_index + 1, lat_devices - 1))),
        ]
    count = len(edges)
    if count == 1:
        facing = jnp.where(is_top, both[1, lat_count - R :], both[1, :R])
    else:
        facing = jnp.concatenate([both[1, :R], both[1, lat_count - R :]])
    even = jnp.concatenate(
        [polar_got[:, :SLAB]] + [e[:, :R] for e in edges] + [polar_got[:, SLAB:]] + [e[:, R : 2 * R] for e in edges], axis=1
    )
    rows = even.shape[1]
    swapped = lax.ppermute(jnp.concatenate([even.reshape((-1,) + even.shape[2:]), facing]), "core", swap)
    odd = swapped[: sectors * rows].reshape(even.shape)
    partner_facing = swapped[sectors * rows :]
    circle = jnp.stack([jnp.where(core == 0, even, odd), jnp.where(core == 0, odd, even)], axis=1)
    circle = circle.reshape((lon_devices,) + even.shape[1:])
    circle = jnp.moveaxis(circle, 0, 1).reshape(rows, lon_total, channels)
    signal_circle, cot_circle = circle[: SLAB + count], circle[SLAB + count :]

    signal_left, signal_right, band_kernel, cycle_kernel, support_width, _ = lax.optimization_barrier(
        (signal_left, signal_right, band_kernel, cycle_kernel, support_width, sent)
    )
    coeffs = band_coefficients(band_kernel, support_width, first_row, total_rows, lat_count + 2 * R)
    forward = band_matrices(coeffs[:, R : R + lat_count], lon_count, True)

    def lag_vector(rows):
        return jnp.concatenate([rows[..., H:], jnp.zeros(rows.shape[:-1] + (lon_total - LAGS,), rows.dtype), rows[..., :H]], -1)

    reads = [coeffs[:, R, 0], coeffs[:, lat_count, 2 * R]]
    gives = [coeffs[:, 0, 2 * R], coeffs[:, lat_count + R, 0]]
    zero = jnp.zeros((K, lon_total), jnp.bfloat16)
    if count == 1:
        edge_forward = lag_vector(jnp.where(is_top, reads[1], reads[0]))[:, None, None]
        edge_adjoint = lag_vector(jnp.where(is_top, gives[1], gives[0]))[:, None, None]
    else:
        edge_forward = block_diagonal(lag_vector(reads[0])[:, None, None], lag_vector(reads[1])[:, None, None])
        edge_adjoint = block_diagonal(lag_vector(gives[0])[:, None, None], lag_vector(gives[1])[:, None, None])
    top_rows = [[cycle_kernel[:, p, s - p + R] if 0 <= s - p + R < TAPS else zero for s in range(SLAB)] for p in range(P_SIZE)]
    low_rows = [[cycle_kernel[:, P_SIZE + p, s - p] if 0 <= s - p < TAPS else zero for s in range(SLAB)] for p in range(P_SIZE)]
    slab_kernel = jnp.where(
        is_top,
        jnp.stack([jnp.stack(row, axis=1) for row in top_rows], axis=1),
        jnp.stack([jnp.stack(row, axis=1) for row in low_rows], axis=1),
    )
    slab_kernel = jnp.where(is_polar, slab_kernel, jnp.zeros_like(slab_kernel))
    def placed(extra, polar_count):
        polar, edge = extra[:, :polar_count], extra[:, polar_count:]

        def rows(block, before):
            return jnp.pad(block, ((0, 0), (before, lat_count - block.shape[1] - before), (0, 0), (0, 0)))

        if count == 1:
            return jnp.where(
                is_top,
                rows(polar, 0) + rows(edge, lat_count - R),
                rows(polar, lat_count - polar_count) + rows(edge, 0),
            )
        out = jnp.where(is_top, rows(polar, 0), rows(polar, lat_count - polar_count))
        return out + rows(edge[:, :R], 0) + rows(edge[:, R:], lat_count - R)

    banded = dot("ikarm,irmc->ikac", forward, windows(signal_left, signal, signal_right))
    banded = bf16(jnp.moveaxis(banded, 1, 0))
    scale = 1.0 / math.sqrt(total_rows * lon_total)
    partial = (dot("kiac,iae->kce", banded, cotangent) * scale).reshape(2, -1, channels)
    given = bf16(jnp.where(core == 0, partial[1], partial[0]))
    kept = jnp.where(core == 0, partial[0], partial[1])
    kept = kept + lax.ppermute(given, "core", swap).astype(jnp.float32)

    slab_kernel, edge_forward, edge_adjoint, _ = lax.optimization_barrier((slab_kernel, edge_forward, edge_adjoint, given))
    lags = jnp.arange(lon_total, dtype=jnp.int32)[:, None, None]
    own_lons = lon_index * lon_count + jnp.arange(lon_count, dtype=jnp.int32)
    chip_lons = chip * 2 * lon_count + jnp.arange(2 * lon_count, dtype=jnp.int32)
    all_lons = jnp.arange(lon_total, dtype=jnp.int32)
    distance = (chip_lons[:, None] - all_lons[None, :]) % lon_total
    opposite = (all_lons[None, :] - own_lons[:, None]) % lon_total
    forward_cycle = bf16(dot("kpsd,dam->kpasm", block_diagonal(slab_kernel, edge_forward), bf16(distance[None] == lags)))
    adjoint_kernel = block_diagonal(jnp.swapaxes(slab_kernel, 1, 2), edge_adjoint)


    extra = dot("kpasm,smc->kpac", forward_cycle, signal_circle)
    chip_polar = lax.dynamic_slice_in_dim(cot_circle[:P_SIZE], chip * 2 * lon_count, 2 * lon_count, 1)
    facing_pair = [jnp.where(core == 0, facing, partner_facing), jnp.where(core == 0, partner_facing, facing)]
    chip_facing = jnp.concatenate(facing_pair, axis=1)
    kept_extra = lax.dynamic_slice_in_dim(bf16(extra), core * (K // 2), K // 2, 0)
    extra_partial = dot("kpac,pae->kce", kept_extra, jnp.concatenate([chip_polar, chip_facing]))
    kept = kept + (extra_partial * scale).reshape(-1, channels)

    group = lat_devices * lon_devices // 2
    parts = lax.all_to_all(bf16(kept).reshape(group, -1, channels), CHIPS, 0, 0)
    chunk = bf16(jnp.sum(parts.astype(jnp.float32), axis=0))
    half = lax.all_to_all(jnp.broadcast_to(chunk[None], (group,) + chunk.shape), CHIPS, 0, 0)
    coeffs, adjoint_kernel, extra, late, kept = lax.optimization_barrier((coeffs, adjoint_kernel, extra, cotangent, kept))
    cot_left, cot_right = sector_edges(late)
    own_extra = lax.dynamic_slice_in_dim(extra, core * lon_count, lon_count, 2)
    filtered = bf16(banded + placed(own_extra, P_SIZE))
    conv_output = bf16(dot("kiac,kce->iae", filtered, weights))

    adjoint_rows = jnp.stack([coeffs[:, t : t + lat_count, 2 * R - t] for t in range(TAPS)], axis=2)
    adjoint = band_matrices(adjoint_rows, lon_count, False)
    adjoint_cycle = bf16(dot("kspd,dbm->ksbpm", adjoint_kernel, bf16(opposite[None] == lags)))
    spread = dot("ikarm,irme->ikae", adjoint, windows(cot_left, cotangent, cot_right))
    spread = jnp.moveaxis(spread, 1, 0)
    spread = spread + placed(dot("ksbpm,pme->ksbe", adjoint_cycle, cot_circle), SLAB)
    signal_grad = bf16(dot("kjbe,kce->jbc", bf16(spread), weights))
    half, conv_output, signal_grad = lax.optimization_barrier((half, conv_output, signal_grad))
    other = lax.ppermute(half, "core", swap)
    weight_grad = jnp.stack([jnp.where(core == 0, half, other), jnp.where(core == 0, other, half)])
    weight_grad = weight_grad.reshape(K, channels, channels).astype(jnp.float32)
    return conv_output, signal_grad, weight_grad


def solution(mesh):
    lat_devices, lon_devices = mesh.devices.shape
    split = Mesh(mesh.devices.reshape(lat_devices, lon_devices // 4, 2, 2), ("lat",) + LON)
    placed = (P("lat", LON, None), P("lat", LON, None), P(), P(), P(), P())
    return jax.shard_map(
        local,
        mesh=split,
        in_specs=placed,
        out_specs=(P("lat", LON, None), P("lat", LON, None), P()),
        check_vma=False,
    )
```

```python
import math

import jax
import jax.numpy as jnp
from jax import lax
from jax.sharding import Mesh, PartitionSpec as P

K = 4
R = 1
H = 8
P_SIZE = 2
TAPS = 2 * R + 1
LAGS = 2 * H + 1
SLAB = P_SIZE + R
LON = ("ring", "pair", "core")
CHIPS = ("lat", "ring", "pair")


def dot(spec, a, b):
    return jnp.einsum(spec, a, b, preferred_element_type=jnp.float32)


def bf16(x):
    return x.astype(jnp.bfloat16)


def band_coefficients(band_kernel, support_width, first_row, total_rows, row_count):
    padded_kernel = jnp.pad(band_kernel, ((0, 0), (R, R), (0, 0), (0, 0)))
    padded_width = jnp.pad(support_width, (R, R))
    kernel_rows = lax.dynamic_slice_in_dim(padded_kernel, first_row, row_count, 1)
    width_rows = lax.dynamic_slice_in_dim(padded_width, first_row, row_count, 0)
    global_rows = first_row - R + jnp.arange(row_count, dtype=jnp.int32)
    polar_rows = (global_rows < P_SIZE) | (global_rows >= total_rows - P_SIZE)
    offsets = jnp.abs(jnp.arange(LAGS, dtype=jnp.int32) - H)
    allowed = (offsets[None, :] <= width_rows[:, None]) & jnp.logical_not(polar_rows)[:, None]
    return jnp.where(allowed[None, :, None, :], kernel_rows, jnp.zeros_like(kernel_rows))


def band_matrices(rows, lon_count, forward):
    outputs = jnp.arange(lon_count, dtype=jnp.int32)[:, None, None]
    inputs = jnp.arange(lon_count + 2 * H, dtype=jnp.int32)[None, :, None]
    shifts = jnp.arange(LAGS, dtype=jnp.int32)[None, None, :]
    table = outputs - inputs + 2 * H == shifts if forward else inputs - outputs == shifts
    return bf16(dot("ktrd,amd->tkarm", rows, bf16(table)))


def windows(left, field, right):
    ext = jnp.concatenate([left, field, right], axis=1)
    ext = jnp.pad(ext, ((R, R), (0, 0), (0, 0)))
    return jnp.stack([ext[t : t + field.shape[0]] for t in range(TAPS)], axis=1)


def block_diagonal(a, b):
    upper = jnp.pad(a, ((0, 0), (0, 0), (0, b.shape[2]), (0, 0)))
    lower = jnp.pad(b, ((0, 0), (0, 0), (a.shape[2], 0), (0, 0)))
    return jnp.concatenate([upper, lower], axis=1)


def local(signal, cotangent, weights, band_kernel, cycle_kernel, support_width):
    lat_count, lon_count, channels = signal.shape
    lat_devices = lax.axis_size("lat")
    lon_devices = lax.axis_size(LON)
    lat_index = lax.axis_index("lat")
    lon_index = lax.axis_index(LON)
    core = lax.axis_index("core")
    chip = lon_index // 2
    lon_total = lon_count * lon_devices
    total_rows = lat_count * lat_devices
    first_row = lat_index * lat_count
    is_top = lat_index == 0
    is_bottom = lat_index == lat_devices - 1
    is_polar = is_top | is_bottom
    swap = [(0, 1), (1, 0)]
    assert lon_count == H

    to_right = [(i, (i + 1) % lon_devices) for i in range(lon_devices)]
    to_left = [(j, i) for i, j in to_right]

    def sector_edges(field):
        return lax.ppermute(field, LON, to_right), lax.ppermute(field, LON, to_left)

    def polar_slab(field, height):
        return lax.dynamic_slice_in_dim(field, jnp.where(is_top, 0, lat_count - height), height, 0)

    signal_left = lax.ppermute(signal, LON, to_right)
    both, after = lax.optimization_barrier((jnp.stack([signal, cotangent]), signal))
    signal_right = lax.ppermute(after, LON, to_left)

    polar_rows = jnp.concatenate([polar_slab(both[0], SLAB), polar_slab(both[1], P_SIZE)])
    fill = jnp.zeros((SLAB + P_SIZE - 2 * R, lon_count, channels), signal.dtype)
    first = jnp.concatenate([both[0, :R], both[1, :R], fill])
    last = jnp.concatenate([both[0, lat_count - R :], both[1, lat_count - R :], fill])
    target = jnp.arange(lat_devices, dtype=jnp.int32)[:, None, None, None]
    chunks = jnp.where(target == lat_index, polar_rows[None], jnp.where(target > lat_index, last[None], first[None]))
    sectors = lon_devices // 2
    sent = jnp.broadcast_to(chunks[:, None], (lat_devices, sectors) + polar_rows.shape)
    got = lax.all_to_all(sent.reshape((-1,) + polar_rows.shape), CHIPS, 0, 0).reshape(sent.shape)

    def from_band(band):
        return lax.dynamic_index_in_dim(got, band, 0, keepdims=False)

    polar_got = from_band(lat_index)
    if lat_devices == 2:
        edges = [from_band(1 - lat_index)]
    else:
        zero_edge = jnp.zeros_like(polar_got)
        edges = [
            jnp.where(is_top, zero_edge, from_band(jnp.maximum(lat_index - 1, 0))),
            jnp.where(is_bottom, zero_edge, from_band(jnp.minimum(lat_index + 1, lat_devices - 1))),
        ]
    count = len(edges)
    if count == 1:
        facing = jnp.where(is_top, both[1, lat_count - R :], both[1, :R])
    else:
        facing = jnp.concatenate([both[1, :R], both[1, lat_count - R :]])
    even = jnp.concatenate(
        [polar_got[:, :SLAB]] + [e[:, :R] for e in edges] + [polar_got[:, SLAB:]] + [e[:, R : 2 * R] for e in edges], axis=1
    )
    rows = even.shape[1]
    swapped = lax.ppermute(jnp.concatenate([even.reshape((-1,) + even.shape[2:]), facing]), "core", swap)
    odd = swapped[: sectors * rows].reshape(even.shape)
    partner_facing = swapped[sectors * rows :]
    circle = jnp.stack([jnp.where(core == 0, even, odd), jnp.where(core == 0, odd, even)], axis=1)
    circle = circle.reshape((lon_devices,) + even.shape[1:])
    circle = jnp.moveaxis(circle, 0, 1).reshape(rows, lon_total, channels)
    signal_circle, cot_circle = circle[: SLAB + count], circle[SLAB + count :]

    signal_left, signal_right, band_kernel, cycle_kernel, support_width, _ = lax.optimization_barrier(
        (signal_left, signal_right, band_kernel, cycle_kernel, support_width, sent)
    )
    coeffs = band_coefficients(band_kernel, support_width, first_row, total_rows, lat_count + 2 * R)
    forward = band_matrices(coeffs[:, R : R + lat_count], lon_count, True)

    def lag_vector(rows):
        return jnp.concatenate([rows[..., H:], jnp.zeros(rows.shape[:-1] + (lon_total - LAGS,), rows.dtype), rows[..., :H]], -1)

    reads = [coeffs[:, R, 0], coeffs[:, lat_count, 2 * R]]
    gives = [coeffs[:, 0, 2 * R], coeffs[:, lat_count + R, 0]]
    zero = jnp.zeros((K, lon_total), jnp.bfloat16)
    if count == 1:
        edge_forward = lag_vector(jnp.where(is_top, reads[1], reads[0]))[:, None, None]
        edge_adjoint = lag_vector(jnp.where(is_top, gives[1], gives[0]))[:, None, None]
    else:
        edge_forward = block_diagonal(lag_vector(reads[0])[:, None, None], lag_vector(reads[1])[:, None, None])
        edge_adjoint = block_diagonal(lag_vector(gives[0])[:, None, None], lag_vector(gives[1])[:, None, None])
    top_rows = [[cycle_kernel[:, p, s - p + R] if 0 <= s - p + R < TAPS else zero for s in range(SLAB)] for p in range(P_SIZE)]
    low_rows = [[cycle_kernel[:, P_SIZE + p, s - p] if 0 <= s - p < TAPS else zero for s in range(SLAB)] for p in range(P_SIZE)]
    slab_kernel = jnp.where(
        is_top,
        jnp.stack([jnp.stack(row, axis=1) for row in top_rows], axis=1),
        jnp.stack([jnp.stack(row, axis=1) for row in low_rows], axis=1),
    )
    slab_kernel = jnp.where(is_polar, slab_kernel, jnp.zeros_like(slab_kernel))
    def placed(extra, polar_count):
        polar, edge = extra[:, :polar_count], extra[:, polar_count:]

        def rows(block, before):
            return jnp.pad(block, ((0, 0), (before, lat_count - block.shape[1] - before), (0, 0), (0, 0)))

        if count == 1:
            return jnp.where(
                is_top,
                rows(polar, 0) + rows(edge, lat_count - R),
                rows(polar, lat_count - polar_count) + rows(edge, 0),
            )
        out = jnp.where(is_top, rows(polar, 0), rows(polar, lat_count - polar_count))
        return out + rows(edge[:, :R], 0) + rows(edge[:, R:], lat_count - R)

    banded = dot("ikarm,irmc->ikac", forward, windows(signal_left, signal, signal_right))
    banded = bf16(jnp.moveaxis(banded, 1, 0))
    scale = 1.0 / math.sqrt(total_rows * lon_total)
    partial = (dot("kiac,iae->kce", banded, cotangent) * scale).reshape(2, -1, channels)
    given = bf16(jnp.where(core == 0, partial[1], partial[0]))
    kept = jnp.where(core == 0, partial[0], partial[1])
    kept = kept + lax.ppermute(given, "core", swap).astype(jnp.float32)

    slab_kernel, edge_forward, edge_adjoint, _ = lax.optimization_barrier((slab_kernel, edge_forward, edge_adjoint, given))
    lags = jnp.arange(lon_total, dtype=jnp.int32)[:, None, None]
    own_lons = lon_index * lon_count + jnp.arange(lon_count, dtype=jnp.int32)
    chip_lons = chip * 2 * lon_count + jnp.arange(2 * lon_count, dtype=jnp.int32)
    all_lons = jnp.arange(lon_total, dtype=jnp.int32)
    distance = (chip_lons[:, None] - all_lons[None, :]) % lon_total
    opposite = (all_lons[None, :] - own_lons[:, None]) % lon_total
    forward_cycle = bf16(dot("kpsd,dam->kpasm", block_diagonal(slab_kernel, edge_forward), bf16(distance[None] == lags)))
    adjoint_kernel = block_diagonal(jnp.swapaxes(slab_kernel, 1, 2), edge_adjoint)


    extra = dot("kpasm,smc->kpac", forward_cycle, signal_circle)
    chip_polar = lax.dynamic_slice_in_dim(cot_circle[:P_SIZE], chip * 2 * lon_count, 2 * lon_count, 1)
    facing_pair = [jnp.where(core == 0, facing, partner_facing), jnp.where(core == 0, partner_facing, facing)]
    chip_facing = jnp.concatenate(facing_pair, axis=1)
    kept_extra = lax.dynamic_slice_in_dim(bf16(extra), core * (K // 2), K // 2, 0)
    extra_partial = dot("kpac,pae->kce", kept_extra, jnp.concatenate([chip_polar, chip_facing]))
    kept = kept + (extra_partial * scale).reshape(-1, channels)

    group = lat_devices * lon_devices // 2
    parts = lax.all_to_all(bf16(kept).reshape(group, -1, channels), CHIPS, 0, 0)
    chunk = bf16(jnp.sum(parts.astype(jnp.float32), axis=0))
    half = lax.all_to_all(jnp.broadcast_to(chunk[None], (group,) + chunk.shape), CHIPS, 0, 0)
    coeffs, adjoint_kernel, extra, late, kept = lax.optimization_barrier((coeffs, adjoint_kernel, extra, cotangent, kept))
    cot_left, cot_right = sector_edges(late)
    own_extra = lax.dynamic_slice_in_dim(extra, core * lon_count, lon_count, 2)
    filtered = bf16(banded + placed(own_extra, P_SIZE))
    conv_output = bf16(dot("kiac,kce->iae", filtered, weights))

    adjoint_rows = jnp.stack([coeffs[:, t : t + lat_count, 2 * R - t] for t in range(TAPS)], axis=2)
    adjoint = band_matrices(adjoint_rows, lon_count, False)
    adjoint_cycle = bf16(dot("kspd,dbm->ksbpm", adjoint_kernel, bf16(opposite[None] == lags)))
    spread = dot("ikarm,irme->ikae", adjoint, windows(cot_left, cotangent, cot_right))
    spread = jnp.moveaxis(spread, 1, 0)
    spread = spread + placed(dot("ksbpm,pme->ksbe", adjoint_cycle, cot_circle), SLAB)
    signal_grad = bf16(dot("kjbe,kce->jbc", bf16(spread), weights))
    half, conv_output, signal_grad = lax.optimization_barrier((half, conv_output, signal_grad))
    other = lax.ppermute(half, "core", swap)
    weight_grad = jnp.stack([jnp.where(core == 0, half, other), jnp.where(core == 0, other, half)])
    weight_grad = weight_grad.reshape(K, channels, channels).astype(jnp.float32)
    return conv_output, signal_grad, weight_grad


def solution(mesh):
    lat_devices, lon_devices = mesh.devices.shape
    split = Mesh(mesh.devices.reshape(lat_devices, lon_devices // 4, 2, 2), ("lat",) + LON)
    placed = (P("lat", LON, None), P("lat", LON, None), P(), P(), P(), P())
    return jax.shard_map(
        local,
        mesh=split,
        in_specs=placed,
        out_specs=(P("lat", LON, None), P("lat", LON, None), P()),
        check_vma=False,
    )
```

```python
import math

import jax
import jax.numpy as jnp
from jax import lax
from jax.sharding import Mesh, PartitionSpec as P

K = 4
R = 1
H = 8
P_SIZE = 2
TAPS = 2 * R + 1
LAGS = 2 * H + 1
SLAB = P_SIZE + R
LON = ("ring", "pair", "core")
CHIPS = ("lat", "ring", "pair")


def dot(spec, a, b):
    return jnp.einsum(spec, a, b, preferred_element_type=jnp.float32)


def bf16(x):
    return x.astype(jnp.bfloat16)


def band_coefficients(band_kernel, support_width, first_row, total_rows, row_count):
    padded_kernel = jnp.pad(band_kernel, ((0, 0), (R, R), (0, 0), (0, 0)))
    padded_width = jnp.pad(support_width, (R, R))
    kernel_rows = lax.dynamic_slice_in_dim(padded_kernel, first_row, row_count, 1)
    width_rows = lax.dynamic_slice_in_dim(padded_width, first_row, row_count, 0)
    global_rows = first_row - R + jnp.arange(row_count, dtype=jnp.int32)
    polar_rows = (global_rows < P_SIZE) | (global_rows >= total_rows - P_SIZE)
    offsets = jnp.abs(jnp.arange(LAGS, dtype=jnp.int32) - H)
    allowed = (offsets[None, :] <= width_rows[:, None]) & jnp.logical_not(polar_rows)[:, None]
    return jnp.where(allowed[None, :, None, :], kernel_rows, jnp.zeros_like(kernel_rows))


def band_matrices(rows, lon_count, forward):
    outputs = jnp.arange(lon_count, dtype=jnp.int32)[:, None, None]
    inputs = jnp.arange(lon_count + 2 * H, dtype=jnp.int32)[None, :, None]
    shifts = jnp.arange(LAGS, dtype=jnp.int32)[None, None, :]
    table = outputs - inputs + 2 * H == shifts if forward else inputs - outputs == shifts
    return bf16(dot("ktrd,amd->tkarm", rows, bf16(table)))


def windows(left, field, right):
    ext = jnp.concatenate([left, field, right], axis=1)
    ext = jnp.pad(ext, ((R, R), (0, 0), (0, 0)))
    return jnp.stack([ext[t : t + field.shape[0]] for t in range(TAPS)], axis=1)


def block_diagonal(a, b):
    upper = jnp.pad(a, ((0, 0), (0, 0), (0, b.shape[2]), (0, 0)))
    lower = jnp.pad(b, ((0, 0), (0, 0), (a.shape[2], 0), (0, 0)))
    return jnp.concatenate([upper, lower], axis=1)


def local(signal, cotangent, weights, band_kernel, cycle_kernel, support_width):
    lat_count, lon_count, channels = signal.shape
    lat_devices = lax.axis_size("lat")
    lon_devices = lax.axis_size(LON)
    lat_index = lax.axis_index("lat")
    lon_index = lax.axis_index(LON)
    core = lax.axis_index("core")
    chip = lon_index // 2
    lon_total = lon_count * lon_devices
    total_rows = lat_count * lat_devices
    first_row = lat_index * lat_count
    is_top = lat_index == 0
    is_bottom = lat_index == lat_devices - 1
    is_polar = is_top | is_bottom
    swap = [(0, 1), (1, 0)]
    assert lon_count == H

    to_right = [(i, (i + 1) % lon_devices) for i in range(lon_devices)]
    to_left = [(j, i) for i, j in to_right]

    def sector_edges(field):
        return lax.ppermute(field, LON, to_right), lax.ppermute(field, LON, to_left)

    def polar_slab(field, height):
        return lax.dynamic_slice_in_dim(field, jnp.where(is_top, 0, lat_count - height), height, 0)

    signal_left = lax.ppermute(signal, LON, to_right)
    both, after = lax.optimization_barrier((jnp.stack([signal, cotangent]), signal))
    signal_right = lax.ppermute(after, LON, to_left)

    polar_rows = jnp.concatenate([polar_slab(both[0], SLAB), polar_slab(both[1], P_SIZE)])
    fill = jnp.zeros((SLAB + P_SIZE - 2 * R, lon_count, channels), signal.dtype)
    first = jnp.concatenate([both[0, :R], both[1, :R], fill])
    last = jnp.concatenate([both[0, lat_count - R :], both[1, lat_count - R :], fill])
    target = jnp.arange(lat_devices, dtype=jnp.int32)[:, None, None, None]
    chunks = jnp.where(target == lat_index, polar_rows[None], jnp.where(target > lat_index, last[None], first[None]))
    sectors = lon_devices // 2
    sent = jnp.broadcast_to(chunks[:, None], (lat_devices, sectors) + polar_rows.shape)
    got = lax.all_to_all(sent.reshape((-1,) + polar_rows.shape), CHIPS, 0, 0).reshape(sent.shape)

    def from_band(band):
        return lax.dynamic_index_in_dim(got, band, 0, keepdims=False)

    polar_got = from_band(lat_index)
    if lat_devices == 2:
        edges = [from_band(1 - lat_index)]
    else:
        zero_edge = jnp.zeros_like(polar_got)
        edges = [
            jnp.where(is_top, zero_edge, from_band(jnp.maximum(lat_index - 1, 0))),
            jnp.where(is_bottom, zero_edge, from_band(jnp.minimum(lat_index + 1, lat_devices - 1))),
        ]
    count = len(edges)
    if count == 1:
        facing = jnp.where(is_top, both[1, lat_count - R :], both[1, :R])
    else:
        facing = jnp.concatenate([both[1, :R], both[1, lat_count - R :]])
    even = jnp.concatenate(
        [polar_got[:, :SLAB]] + [e[:, :R] for e in edges] + [polar_got[:, SLAB:]] + [e[:, R : 2 * R] for e in edges], axis=1
    )
    rows = even.shape[1]
    swapped = lax.ppermute(jnp.concatenate([even.reshape((-1,) + even.shape[2:]), facing]), "core", swap)
    odd = swapped[: sectors * rows].reshape(even.shape)
    partner_facing = swapped[sectors * rows :]
    circle = jnp.stack([jnp.where(core == 0, even, odd), jnp.where(core == 0, odd, even)], axis=1)
    circle = circle.reshape((lon_devices,) + even.shape[1:])
    circle = jnp.moveaxis(circle, 0, 1).reshape(rows, lon_total, channels)
    signal_circle, cot_circle = circle[: SLAB + count], circle[SLAB + count :]

    signal_left, signal_right, band_kernel, cycle_kernel, support_width, _ = lax.optimization_barrier(
        (signal_left, signal_right, band_kernel, cycle_kernel, support_width, sent)
    )
    coeffs = band_coefficients(band_kernel, support_width, first_row, total_rows, lat_count + 2 * R)
    forward = band_matrices(coeffs[:, R : R + lat_count], lon_count, True)

    def lag_vector(rows):
        return jnp.concatenate([rows[..., H:], jnp.zeros(rows.shape[:-1] + (lon_total - LAGS,), rows.dtype), rows[..., :H]], -1)

    reads = [coeffs[:, R, 0], coeffs[:, lat_count, 2 * R]]
    gives = [coeffs[:, 0, 2 * R], coeffs[:, lat_count + R, 0]]
    zero = jnp.zeros((K, lon_total), jnp.bfloat16)
    if count == 1:
        edge_forward = lag_vector(jnp.where(is_top, reads[1], reads[0]))[:, None, None]
        edge_adjoint = lag_vector(jnp.where(is_top, gives[1], gives[0]))[:, None, None]
    else:
        edge_forward = block_diagonal(lag_vector(reads[0])[:, None, None], lag_vector(reads[1])[:, None, None])
        edge_adjoint = block_diagonal(lag_vector(gives[0])[:, None, None], lag_vector(gives[1])[:, None, None])
    top_rows = [[cycle_kernel[:, p, s - p + R] if 0 <= s - p + R < TAPS else zero for s in range(SLAB)] for p in range(P_SIZE)]
    low_rows = [[cycle_kernel[:, P_SIZE + p, s - p] if 0 <= s - p < TAPS else zero for s in range(SLAB)] for p in range(P_SIZE)]
    slab_kernel = jnp.where(
        is_top,
        jnp.stack([jnp.stack(row, axis=1) for row in top_rows], axis=1),
        jnp.stack([jnp.stack(row, axis=1) for row in low_rows], axis=1),
    )
    slab_kernel = jnp.where(is_polar, slab_kernel, jnp.zeros_like(slab_kernel))
    def placed(extra, polar_count):
        polar, edge = extra[:, :polar_count], extra[:, polar_count:]

        def rows(block, before):
            return jnp.pad(block, ((0, 0), (before, lat_count - block.shape[1] - before), (0, 0), (0, 0)))

        if count == 1:
            return jnp.where(
                is_top,
                rows(polar, 0) + rows(edge, lat_count - R),
                rows(polar, lat_count - polar_count) + rows(edge, 0),
            )
        out = jnp.where(is_top, rows(polar, 0), rows(polar, lat_count - polar_count))
        return out + rows(edge[:, :R], 0) + rows(edge[:, R:], lat_count - R)

    banded = dot("ikarm,irmc->ikac", forward, windows(signal_left, signal, signal_right))
    banded = bf16(jnp.moveaxis(banded, 1, 0))
    scale = 1.0 / math.sqrt(total_rows * lon_total)
    partial = (dot("kiac,iae->kce", banded, cotangent) * scale).reshape(2, -1, channels)
    given = bf16(jnp.where(core == 0, partial[1], partial[0]))
    kept = jnp.where(core == 0, partial[0], partial[1])
    given, late = lax.optimization_barrier((given, cotangent))
    cot_left, cot_right = sector_edges(late)
    kept = kept + lax.ppermute(given, "core", swap).astype(jnp.float32)

    slab_kernel, edge_forward, edge_adjoint, _ = lax.optimization_barrier((slab_kernel, edge_forward, edge_adjoint, given))
    lags = jnp.arange(lon_total, dtype=jnp.int32)[:, None, None]
    own_lons = lon_index * lon_count + jnp.arange(lon_count, dtype=jnp.int32)
    chip_lons = chip * 2 * lon_count + jnp.arange(2 * lon_count, dtype=jnp.int32)
    all_lons = jnp.arange(lon_total, dtype=jnp.int32)
    distance = (chip_lons[:, None] - all_lons[None, :]) % lon_total
    opposite = (all_lons[None, :] - own_lons[:, None]) % lon_total
    forward_cycle = bf16(dot("kpsd,dam->kpasm", block_diagonal(slab_kernel, edge_forward), bf16(distance[None] == lags)))
    adjoint_kernel = block_diagonal(jnp.swapaxes(slab_kernel, 1, 2), edge_adjoint)


    extra = dot("kpasm,smc->kpac", forward_cycle, signal_circle)
    chip_polar = lax.dynamic_slice_in_dim(cot_circle[:P_SIZE], chip * 2 * lon_count, 2 * lon_count, 1)
    facing_pair = [jnp.where(core == 0, facing, partner_facing), jnp.where(core == 0, partner_facing, facing)]
    chip_facing = jnp.concatenate(facing_pair, axis=1)
    kept_extra = lax.dynamic_slice_in_dim(bf16(extra), core * (K // 2), K // 2, 0)
    extra_partial = dot("kpac,pae->kce", kept_extra, jnp.concatenate([chip_polar, chip_facing]))
    kept = kept + (extra_partial * scale).reshape(-1, channels)

    group = lat_devices * lon_devices // 2
    parts = lax.all_to_all(bf16(kept).reshape(group, -1, channels), CHIPS, 0, 0)
    chunk = bf16(jnp.sum(parts.astype(jnp.float32), axis=0))
    half = lax.all_to_all(jnp.broadcast_to(chunk[None], (group,) + chunk.shape), CHIPS, 0, 0)
    coeffs, adjoint_kernel, extra, kept = lax.optimization_barrier((coeffs, adjoint_kernel, extra, kept))
    own_extra = lax.dynamic_slice_in_dim(extra, core * lon_count, lon_count, 2)
    filtered = bf16(banded + placed(own_extra, P_SIZE))
    conv_output = bf16(dot("kiac,kce->iae", filtered, weights))

    adjoint_rows = jnp.stack([coeffs[:, t : t + lat_count, 2 * R - t] for t in range(TAPS)], axis=2)
    adjoint = band_matrices(adjoint_rows, lon_count, False)
    adjoint_cycle = bf16(dot("kspd,dbm->ksbpm", adjoint_kernel, bf16(opposite[None] == lags)))
    cot_left, cot_right, _ = lax.optimization_barrier((cot_left, cot_right, chunk))
    spread = dot("ikarm,irme->ikae", adjoint, windows(cot_left, cotangent, cot_right))
    spread = jnp.moveaxis(spread, 1, 0)
    spread = spread + placed(dot("ksbpm,pme->ksbe", adjoint_cycle, cot_circle), SLAB)
    signal_grad = bf16(dot("kjbe,kce->jbc", bf16(spread), weights))
    half, conv_output, signal_grad = lax.optimization_barrier((half, conv_output, signal_grad))
    other = lax.ppermute(half, "core", swap)
    weight_grad = jnp.stack([jnp.where(core == 0, half, other), jnp.where(core == 0, other, half)])
    weight_grad = weight_grad.reshape(K, channels, channels).astype(jnp.float32)
    return conv_output, signal_grad, weight_grad


def solution(mesh):
    lat_devices, lon_devices = mesh.devices.shape
    split = Mesh(mesh.devices.reshape(lat_devices, lon_devices // 4, 2, 2), ("lat",) + LON)
    placed = (P("lat", LON, None), P("lat", LON, None), P(), P(), P(), P())
    return jax.shard_map(
        local,
        mesh=split,
        in_specs=placed,
        out_specs=(P("lat", LON, None), P("lat", LON, None), P()),
        check_vma=False,
    )
```

```python
import math

import jax
import jax.numpy as jnp
from jax import lax
from jax.sharding import Mesh, PartitionSpec as P

K = 4
R = 1
H = 8
P_SIZE = 2
TAPS = 2 * R + 1
LAGS = 2 * H + 1
SLAB = P_SIZE + R
LON = ("ring", "pair", "core")
CHIPS = ("lat", "ring", "pair")


def dot(spec, a, b):
    return jnp.einsum(spec, a, b, preferred_element_type=jnp.float32)


def bf16(x):
    return x.astype(jnp.bfloat16)


def band_coefficients(band_kernel, support_width, first_row, total_rows, row_count):
    padded_kernel = jnp.pad(band_kernel, ((0, 0), (R, R), (0, 0), (0, 0)))
    padded_width = jnp.pad(support_width, (R, R))
    kernel_rows = lax.dynamic_slice_in_dim(padded_kernel, first_row, row_count, 1)
    width_rows = lax.dynamic_slice_in_dim(padded_width, first_row, row_count, 0)
    global_rows = first_row - R + jnp.arange(row_count, dtype=jnp.int32)
    polar_rows = (global_rows < P_SIZE) | (global_rows >= total_rows - P_SIZE)
    offsets = jnp.abs(jnp.arange(LAGS, dtype=jnp.int32) - H)
    allowed = (offsets[None, :] <= width_rows[:, None]) & jnp.logical_not(polar_rows)[:, None]
    return jnp.where(allowed[None, :, None, :], kernel_rows, jnp.zeros_like(kernel_rows))


def band_matrices(rows, lon_count, forward):
    outputs = jnp.arange(lon_count, dtype=jnp.int32)[:, None, None]
    inputs = jnp.arange(lon_count + 2 * H, dtype=jnp.int32)[None, :, None]
    shifts = jnp.arange(LAGS, dtype=jnp.int32)[None, None, :]
    table = outputs - inputs + 2 * H == shifts if forward else inputs - outputs == shifts
    return bf16(dot("ktrd,amd->tkarm", rows, bf16(table)))


def windows(left, field, right):
    ext = jnp.concatenate([left, field, right], axis=1)
    ext = jnp.pad(ext, ((R, R), (0, 0), (0, 0)))
    return jnp.stack([ext[t : t + field.shape[0]] for t in range(TAPS)], axis=1)


def block_diagonal(a, b):
    upper = jnp.pad(a, ((0, 0), (0, 0), (0, b.shape[2]), (0, 0)))
    lower = jnp.pad(b, ((0, 0), (0, 0), (a.shape[2], 0), (0, 0)))
    return jnp.concatenate([upper, lower], axis=1)


def local(signal, cotangent, weights, band_kernel, cycle_kernel, support_width):
    lat_count, lon_count, channels = signal.shape
    lat_devices = lax.axis_size("lat")
    lon_devices = lax.axis_size(LON)
    lat_index = lax.axis_index("lat")
    lon_index = lax.axis_index(LON)
    core = lax.axis_index("core")
    chip = lon_index // 2
    lon_total = lon_count * lon_devices
    total_rows = lat_count * lat_devices
    first_row = lat_index * lat_count
    is_top = lat_index == 0
    is_bottom = lat_index == lat_devices - 1
    is_polar = is_top | is_bottom
    swap = [(0, 1), (1, 0)]
    assert lon_count == H

    to_right = [(i, (i + 1) % lon_devices) for i in range(lon_devices)]
    to_left = [(j, i) for i, j in to_right]

    def sector_edges(field):
        return lax.ppermute(field, LON, to_right), lax.ppermute(field, LON, to_left)

    def polar_slab(field, height):
        return lax.dynamic_slice_in_dim(field, jnp.where(is_top, 0, lat_count - height), height, 0)

    signal_left, signal_right = sector_edges(signal)

    polar_rows = jnp.concatenate([polar_slab(signal, SLAB), polar_slab(cotangent, P_SIZE)])
    fill = jnp.zeros((SLAB + P_SIZE - 2 * R, lon_count, channels), signal.dtype)
    first = jnp.concatenate([signal[:R], cotangent[:R], fill])
    last = jnp.concatenate([signal[lat_count - R :], cotangent[lat_count - R :], fill])
    target = jnp.arange(lat_devices, dtype=jnp.int32)[:, None, None, None]
    chunks = jnp.where(target == lat_index, polar_rows[None], jnp.where(target > lat_index, last[None], first[None]))
    sectors = lon_devices // 2
    sent = jnp.broadcast_to(chunks[:, None], (lat_devices, sectors) + polar_rows.shape)
    got = lax.all_to_all(sent.reshape((-1,) + polar_rows.shape), CHIPS, 0, 0).reshape(sent.shape)

    def from_band(band):
        return lax.dynamic_index_in_dim(got, band, 0, keepdims=False)

    polar_got = from_band(lat_index)
    if lat_devices == 2:
        edges = [from_band(1 - lat_index)]
    else:
        zero_edge = jnp.zeros_like(polar_got)
        edges = [
            jnp.where(is_top, zero_edge, from_band(jnp.maximum(lat_index - 1, 0))),
            jnp.where(is_bottom, zero_edge, from_band(jnp.minimum(lat_index + 1, lat_devices - 1))),
        ]
    count = len(edges)
    if count == 1:
        facing = jnp.where(is_top, cotangent[lat_count - R :], cotangent[:R])
    else:
        facing = jnp.concatenate([cotangent[:R], cotangent[lat_count - R :]])
    even = jnp.concatenate(
        [polar_got[:, :SLAB]] + [e[:, :R] for e in edges] + [polar_got[:, SLAB:]] + [e[:, R : 2 * R] for e in edges], axis=1
    )
    rows = even.shape[1]
    swapped = lax.ppermute(jnp.concatenate([even.reshape((-1,) + even.shape[2:]), facing]), "core", swap)
    odd = swapped[: sectors * rows].reshape(even.shape)
    partner_facing = swapped[sectors * rows :]
    circle = jnp.stack([jnp.where(core == 0, even, odd), jnp.where(core == 0, odd, even)], axis=1)
    circle = circle.reshape((lon_devices,) + even.shape[1:])
    circle = jnp.moveaxis(circle, 0, 1).reshape(rows, lon_total, channels)
    signal_circle, cot_circle = circle[: SLAB + count], circle[SLAB + count :]

    signal_left, signal_right, band_kernel, cycle_kernel, support_width, _ = lax.optimization_barrier(
        (signal_left, signal_right, band_kernel, cycle_kernel, support_width, sent)
    )
    coeffs = band_coefficients(band_kernel, support_width, first_row, total_rows, lat_count + 2 * R)
    forward = band_matrices(coeffs[:, R : R + lat_count], lon_count, True)

    def lag_vector(rows):
        return jnp.concatenate([rows[..., H:], jnp.zeros(rows.shape[:-1] + (lon_total - LAGS,), rows.dtype), rows[..., :H]], -1)

    reads = [coeffs[:, R, 0], coeffs[:, lat_count, 2 * R]]
    gives = [coeffs[:, 0, 2 * R], coeffs[:, lat_count + R, 0]]
    zero = jnp.zeros((K, lon_total), jnp.bfloat16)
    if count == 1:
        edge_forward = lag_vector(jnp.where(is_top, reads[1], reads[0]))[:, None, None]
        edge_adjoint = lag_vector(jnp.where(is_top, gives[1], gives[0]))[:, None, None]
    else:
        edge_forward = block_diagonal(lag_vector(reads[0])[:, None, None], lag_vector(reads[1])[:, None, None])
        edge_adjoint = block_diagonal(lag_vector(gives[0])[:, None, None], lag_vector(gives[1])[:, None, None])
    top_rows = [[cycle_kernel[:, p, s - p + R] if 0 <= s - p + R < TAPS else zero for s in range(SLAB)] for p in range(P_SIZE)]
    low_rows = [[cycle_kernel[:, P_SIZE + p, s - p] if 0 <= s - p < TAPS else zero for s in range(SLAB)] for p in range(P_SIZE)]
    slab_kernel = jnp.where(
        is_top,
        jnp.stack([jnp.stack(row, axis=1) for row in top_rows], axis=1),
        jnp.stack([jnp.stack(row, axis=1) for row in low_rows], axis=1),
    )
    slab_kernel = jnp.where(is_polar, slab_kernel, jnp.zeros_like(slab_kernel))
    lags = jnp.arange(lon_total, dtype=jnp.int32)[:, None, None]
    own_lons = lon_index * lon_count + jnp.arange(lon_count, dtype=jnp.int32)
    chip_lons = chip * 2 * lon_count + jnp.arange(2 * lon_count, dtype=jnp.int32)
    all_lons = jnp.arange(lon_total, dtype=jnp.int32)
    distance = (chip_lons[:, None] - all_lons[None, :]) % lon_total
    opposite = (all_lons[None, :] - own_lons[:, None]) % lon_total
    forward_cycle = bf16(dot("kpsd,dam->kpasm", block_diagonal(slab_kernel, edge_forward), bf16(distance[None] == lags)))
    adjoint_kernel = block_diagonal(jnp.swapaxes(slab_kernel, 1, 2), edge_adjoint)

    def placed(extra, polar_count):
        polar, edge = extra[:, :polar_count], extra[:, polar_count:]

        def rows(block, before):
            return jnp.pad(block, ((0, 0), (before, lat_count - block.shape[1] - before), (0, 0), (0, 0)))

        if count == 1:
            return jnp.where(
                is_top,
                rows(polar, 0) + rows(edge, lat_count - R),
                rows(polar, lat_count - polar_count) + rows(edge, 0),
            )
        out = jnp.where(is_top, rows(polar, 0), rows(polar, lat_count - polar_count))
        return out + rows(edge[:, :R], 0) + rows(edge[:, R:], lat_count - R)

    banded = dot("ikarm,irmc->ikac", forward, windows(signal_left, signal, signal_right))
    banded = bf16(jnp.moveaxis(banded, 1, 0))
    scale = 1.0 / math.sqrt(total_rows * lon_total)
    partial = (dot("kiac,iae->kce", banded, cotangent) * scale).reshape(2, -1, channels)
    given = bf16(jnp.where(core == 0, partial[1], partial[0]))
    kept = jnp.where(core == 0, partial[0], partial[1])
    given, late = lax.optimization_barrier((given, cotangent))
    cot_left, cot_right = sector_edges(late)
    kept = kept + lax.ppermute(given, "core", swap).astype(jnp.float32)

    extra = dot("kpasm,smc->kpac", forward_cycle, signal_circle)
    chip_polar = lax.dynamic_slice_in_dim(cot_circle[:P_SIZE], chip * 2 * lon_count, 2 * lon_count, 1)
    facing_pair = [jnp.where(core == 0, facing, partner_facing), jnp.where(core == 0, partner_facing, facing)]
    chip_facing = jnp.concatenate(facing_pair, axis=1)
    kept_extra = lax.dynamic_slice_in_dim(bf16(extra), core * (K // 2), K // 2, 0)
    extra_partial = dot("kpac,pae->kce", kept_extra, jnp.concatenate([chip_polar, chip_facing]))
    kept = kept + (extra_partial * scale).reshape(-1, channels)

    group = lat_devices * lon_devices // 2
    parts = lax.all_to_all(bf16(kept).reshape(group, -1, channels), CHIPS, 0, 0)
    chunk = bf16(jnp.sum(parts.astype(jnp.float32), axis=0))
    half = lax.all_to_all(jnp.broadcast_to(chunk[None], (group,) + chunk.shape), CHIPS, 0, 0)
    coeffs, adjoint_kernel, extra, kept = lax.optimization_barrier((coeffs, adjoint_kernel, extra, kept))
    own_extra = lax.dynamic_slice_in_dim(extra, core * lon_count, lon_count, 2)
    filtered = bf16(banded + placed(own_extra, P_SIZE))
    conv_output = bf16(dot("kiac,kce->iae", filtered, weights))

    adjoint_rows = jnp.stack([coeffs[:, t : t + lat_count, 2 * R - t] for t in range(TAPS)], axis=2)
    adjoint = band_matrices(adjoint_rows, lon_count, False)
    adjoint_cycle = bf16(dot("kspd,dbm->ksbpm", adjoint_kernel, bf16(opposite[None] == lags)))
    cot_left, cot_right, _ = lax.optimization_barrier((cot_left, cot_right, chunk))
    spread = dot("ikarm,irme->ikae", adjoint, windows(cot_left, cotangent, cot_right))
    spread = jnp.moveaxis(spread, 1, 0)
    spread = spread + placed(dot("ksbpm,pme->ksbe", adjoint_cycle, cot_circle), SLAB)
    signal_grad = bf16(dot("kjbe,kce->jbc", bf16(spread), weights))
    half, conv_output, signal_grad = lax.optimization_barrier((half, conv_output, signal_grad))
    other = lax.ppermute(half, "core", swap)
    weight_grad = jnp.stack([jnp.where(core == 0, half, other), jnp.where(core == 0, other, half)])
    weight_grad = weight_grad.reshape(K, channels, channels).astype(jnp.float32)
    return conv_output, signal_grad, weight_grad


def solution(mesh):
    lat_devices, lon_devices = mesh.devices.shape
    split = Mesh(mesh.devices.reshape(lat_devices, lon_devices // 4, 2, 2), ("lat",) + LON)
    placed = (P("lat", LON, None), P("lat", LON, None), P(), P(), P(), P())
    return jax.shard_map(
        local,
        mesh=split,
        in_specs=placed,
        out_specs=(P("lat", LON, None), P("lat", LON, None), P()),
        check_vma=False,
    )
```
